256 devices in a mesh: group: 16 (over y_lo, x, core), peer: 16 (over y_hi, z).
Axes of the slice: x: 4, y: 4 (y_hi: 2, y_lo: 2; y = y_hi * 2 + y_lo), z: 8, core: 2. Of those that a mesh axis runs over, the one named last changes fastest.
Arguments:
- dense_feat: bfloat16 [98304, 128], P(('group', 'peer')), may hold values from -6 to 6
- upstream: bfloat16 [98304, 3456], P(('group', 'peer')), may hold values from -0.078125 to 0.078125
- cur_ids: int32 [98304, 26], P(('group', 'peer')), may hold values from 0 to 2047
- work_rows: float32 [524288, 128], P(('group', 'peer')), may hold values from -6 to 6
- work_acc: float32 [524288], P(('group', 'peer')), may hold values from 1.0172526e-05 to 0.00010172526
- cache_table: float32 [131072, 128], P(('group', 'peer')), may hold values from -6 to 6
- home_table: float32 [262144, 128], P(('group', 'peer')), may hold values from -6 to 6
- hit_send: int32 [4096, 64], P(('group', 'peer')), may hold values from 0 to 511
- hit_count: int32 [4096], P(('group', 'peer')), may hold values from 8 to 64, as said below
- miss_send: int32 [4096, 64], P(('group', 'peer')), may hold values from 0 to 1023
- miss_count: int32 [4096], P(('group', 'peer')), may hold values from 8 to 64, as said below
- evict_slot: int32 [4096, 32], P(('group', 'peer')), may hold values from 0 to 2047
- evict_dest: int32 [4096, 32], P(('group', 'peer')), may hold values from 0 to 1023
- evict_count: int32 [4096], P(('group', 'peer')), may hold values from 4 to 32, as said below
- up_proj: bfloat16 [3456, 256], replicated, may hold values from -0.109375 to 0.109375
- down_proj: bfloat16 [256, 3456], replicated, may hold values from -0.375 to 0.375
- cross_bias: float32 [3456], replicated, may hold values from -3 to 3
Outputs:
- next_work: float32 [524288, 128], P(('group', 'peer'))
- work_new: float32 [524288, 128], P(('group', 'peer'))
- home_new: float32 [262144, 128], P(('group', 'peer'))
- grad_up: float32 [3456, 256], P('peer')
- grad_down: float32 [256, 3456], P('peer')
- grad_bias: float32 [3456], P('peer')
The draws below stay inside these ranges and needn't reach their ends.
Inputs may be any that keep to these rules, and one draw needn't show every extreme that they name: `hit_count`: in every group some peer receives the full 64 rows from every holder of the group. `miss_count`: for every peer index some group receives the full 64 rows from that peer index of every group. `evict_count`: for every peer index some home group receives the full 32 rows from that peer index of every group.
All inputs are finite; a program needn't handle non-finite values.
Results may differ from the reference program's by a relative error of at most 0.007.
Values sent between devices are 32-bit elements; how exact they have to be, the bound alone decides.
A program may use at most 128 MiB of HBM per device.

```python
import math
import jax
import jax.numpy as jnp
import numpy as np
from jax import lax

ROW_WIDTH = 128
FEATURES = 26
LOW_RANK = 256
BATCH_DEV = 384
HOME_ROWS = 1024
CACHE_ROWS = 512
HIT_CAP = 64
MISS_CAP = 64
EVICT_CAP = 32
CROSS_WIDTH = 3456
WORK_SET = 2048
SAMPLES = 98304
N_GROUP = 16
N_PEER = 16
DEVICES = 256


def capped_counts(key, senders, middle, dests, cap, pick_shape, pick_range):
    lower = jax.random.randint(jax.random.fold_in(key, 5), (senders, middle, dests), cap // 8, cap + 1)
    target = jax.random.randint(jax.random.fold_in(key, 6), pick_shape, 0, pick_range)
    column = jnp.arange(dests).reshape(1, 1, dests)
    return jnp.where(column == target, cap, lower).reshape(-1).astype(jnp.int32)


def draw_hit_count(key, part):
    key = jax.random.fold_in(key, 1)
    return capped_counts(key, N_GROUP, N_PEER, N_PEER, HIT_CAP, (N_GROUP, 1, 1), N_PEER)


def draw_miss_count(key, part):
    key = jax.random.fold_in(key, 2)
    return capped_counts(key, N_GROUP, N_PEER, N_GROUP, MISS_CAP, (1, N_PEER, 1), N_GROUP)


def draw_evict_count(key, part):
    key = jax.random.fold_in(key, 3)
    return capped_counts(key, N_GROUP, N_PEER, N_GROUP, EVICT_CAP, (1, N_PEER, 1), N_GROUP)


def set_ends(drawn, own_key, low, largest):
    extent = drawn.shape
    spot = [jax.random.randint(jax.random.fold_in(own_key, axis), (), 0, extent[axis]) for axis in range(len(extent))]
    drawn = drawn.at[tuple(spot)].set(low)
    longest = extent.index(max(extent))
    spot[longest] = (spot[longest] + 1) % extent[longest]
    return drawn.at[tuple(spot)].set(largest)


def raised(entries, rng, source, target, shards_of, factor):
    def block_of(position):
        return (jnp.arange(entries.shape[position]) // (entries.shape[position] // shards_of)).reshape((-1,) + (1,) * (entries.ndim - 1 - position))

    one_side = jax.random.permutation(rng, shards_of)[block_of(target)]
    second = (block_of(target) + shards_of // 2) % shards_of
    return jnp.where((block_of(source) == one_side) | (block_of(source) == second), factor * entries, entries)


def block_scale(stream_key, dims, shards, least, top_value):
    level, own = 1.0, jax.random.fold_in(stream_key, 6)
    for dim, parts in shards:
        draws = jnp.exp(jax.random.uniform(jax.random.fold_in(own, dim), (parts,), jnp.float32, least / len(shards), top_value / len(shards)))
        level = level * jnp.repeat(draws, dims[dim] // parts).reshape([-1 if axis == dim else 1 for axis in range(len(dims))])
    return level


def rank_table(amount, skew):
    loads = [(1 << 20) // math.isqrt(grade ** skew) + 1 for grade in range(1, amount + 1)]
    scale = 1 + sum(loads) // (1 << 30)
    return np.cumsum(np.array([max(1, weight // scale) for weight in loads]))


def ranked_ids(own_key, shape, count, lean):
    table = rank_table(count, lean)
    lot = jax.random.randint(jax.random.fold_in(own_key, 1), shape, 0, int(table[count - 1]))
    standing = jnp.searchsorted(jnp.asarray(table, jnp.int32), lot, side="right")
    return jax.random.permutation(jax.random.fold_in(own_key, 2), count)[standing].astype(jnp.int32)


def centred(key, dims, spread, most, pieces=(), kind=jnp.bfloat16):
    array = jax.random.normal(key, dims, jnp.float32) * spread
    if len(pieces) > 0:
        array = block_scale(key, dims, pieces, -0.22, 0.18) * array
    return jnp.clip(array, min=-most, max=most).astype(kind)


def gaussian_with(rng, shape, width, most, split, heavy, held_as=jnp.bfloat16):
    drawn = width * jax.random.normal(rng, shape, jnp.float32)
    if split:
        drawn = drawn * block_scale(rng, shape, split, -0.22, 0.18)
    return jnp.clip(raised(drawn, jax.random.fold_in(rng, 3), *heavy), -most, most).astype(held_as)


def setup_inputs(seed: int = 0) -> dict:
    streams_of = jax.random.split(jax.random.key(seed), 18)
    return {
        "dense_feat": centred(streams_of[0], (SAMPLES, ROW_WIDTH), 1.0, 6.0, ((0, 256),)),
        "upstream": gaussian_with(streams_of[1], (SAMPLES, CROSS_WIDTH), (1 / SAMPLES ** 0.5), 0.078125, ((0, 256),), (0, 1, 128, 5.5)),
        "cur_ids": set_ends(ranked_ids(streams_of[2], (SAMPLES, FEATURES), WORK_SET, 2), jax.random.fold_in(streams_of[2], 3), 0, WORK_SET - 1).astype(jnp.int32),
        "work_rows": centred(streams_of[3], (WORK_SET * DEVICES, ROW_WIDTH), 1.0, 6.0, ((0, 256),), jnp.float32),
        "work_acc": jnp.clip(jnp.exp(math.log(0.00010172526) - 2.30258504 * jax.random.uniform(streams_of[4], (WORK_SET * DEVICES,), jnp.float32) ** block_scale(streams_of[4], (WORK_SET * DEVICES,), ((0, 256),), -0.2, 0.2)), 1.0172526344831567e-05, 0.00010172526),
        "cache_table": centred(streams_of[5], (CACHE_ROWS * DEVICES, ROW_WIDTH), 1.0, 6.0, ((0, 256),), jnp.float32),
        "home_table": centred(streams_of[6], (HOME_ROWS * DEVICES, ROW_WIDTH), 1.0, 6.0, ((0, 256),), jnp.float32),
        "hit_send": set_ends(jax.random.randint(streams_of[7], (DEVICES * N_PEER, HIT_CAP), 0, CACHE_ROWS), jax.random.fold_in(streams_of[7], 1), 0, CACHE_ROWS - 1).astype(jnp.int32),
        "hit_count": draw_hit_count(jax.random.fold_in(streams_of[17], 71), 0),
        "miss_send": set_ends(jax.random.randint(streams_of[9], (DEVICES * N_GROUP, MISS_CAP), 0, HOME_ROWS), jax.random.fold_in(streams_of[9], 1), 0, HOME_ROWS - 1).astype(jnp.int32),
        "miss_count": draw_miss_count(jax.random.fold_in(streams_of[17], 71), 0),
        "evict_slot": set_ends(jax.random.randint(streams_of[11], (DEVICES * N_GROUP, EVICT_CAP), 0, WORK_SET), jax.random.fold_in(streams_of[11], 1), 0, WORK_SET - 1).astype(jnp.int32),
        "evict_dest": set_ends(jax.random.randint(streams_of[12], (DEVICES * N_GROUP, EVICT_CAP), 0, HOME_ROWS), jax.random.fold_in(streams_of[12], 1), 0, HOME_ROWS - 1).astype(jnp.int32),
        "evict_count": draw_evict_count(jax.random.fold_in(streams_of[17], 71), 0),
        "up_proj": centred(streams_of[14], (CROSS_WIDTH, LOW_RANK), CROSS_WIDTH ** -0.5, 0.109375),
        "down_proj": centred(streams_of[15], (LOW_RANK, CROSS_WIDTH), LOW_RANK ** -0.5, 0.375),
        "cross_bias": centred(streams_of[16], (CROSS_WIDTH,), 0.5, 3.0, (), jnp.float32),
    }


step_size = 0.5

def masked_rows(table, listed, counts):
    picked = table[listed]
    keep = jnp.arange(listed.shape[-1])[None, :] < counts[:, None]
    return jnp.where(keep[:, :, None], picked, jnp.zeros_like(picked))

def reference(dense_feat, upstream, cur_ids, work_rows, work_acc, cache_table, home_table, hit_send, hit_count, miss_send, miss_count, evict_slot, evict_dest, evict_count, up_proj, down_proj, cross_bias):
    ndevices = N_GROUP * N_PEER

    def device_grads(running, inputs):
        grad_up, grad_down, grad_bias = running
        dense_block, upstream_block, id_block, row_block, acc_block = inputs
        flat_ids = id_block.reshape(-1).astype(jnp.int32)
        looked = row_block[flat_ids].reshape(BATCH_DEV, FEATURES * ROW_WIDTH).astype(jnp.bfloat16)
        stacked = jnp.concatenate([dense_block, looked], axis=1)
        hidden = jnp.dot(stacked, up_proj, preferred_element_type=jnp.float32).astype(jnp.bfloat16)
        cross_out = jnp.dot(hidden, down_proj, preferred_element_type=jnp.float32) + cross_bias
        gated = (upstream_block.astype(jnp.float32) * stacked.astype(jnp.float32)).astype(jnp.bfloat16)
        grad_down = grad_down + jnp.dot(hidden.T, gated, preferred_element_type=jnp.float32)
        grad_bias = grad_bias + lax.optimization_barrier(jnp.sum(gated.astype(jnp.float32), axis=0))
        back_hidden = jnp.dot(gated, down_proj.T, preferred_element_type=jnp.float32).astype(jnp.bfloat16)
        grad_up = grad_up + jnp.dot(stacked.T, back_hidden, preferred_element_type=jnp.float32)
        grad_input = upstream_block.astype(jnp.float32) * (cross_out + 1.0) + jnp.dot(back_hidden, up_proj.T, preferred_element_type=jnp.float32)
        row_terms = grad_input[:, ROW_WIDTH:].reshape(-1, ROW_WIDTH)
        row_grads = jnp.zeros((WORK_SET, ROW_WIDTH), jnp.float32).at[flat_ids].add(row_terms)
        acc_new = acc_block + lax.optimization_barrier(jnp.mean(row_grads * row_grads, axis=1))
        row_delta = -step_size * row_grads / jnp.sqrt(acc_new)[:, None]
        return ((grad_up, grad_down, grad_bias), row_delta)
    start = (jnp.zeros((CROSS_WIDTH, LOW_RANK), jnp.float32), jnp.zeros((LOW_RANK, CROSS_WIDTH), jnp.float32), jnp.zeros((CROSS_WIDTH,), jnp.float32))
    inputs = (dense_feat.reshape(ndevices, BATCH_DEV, ROW_WIDTH), upstream.reshape(ndevices, BATCH_DEV, CROSS_WIDTH), cur_ids.reshape(ndevices, BATCH_DEV, FEATURES), work_rows.reshape(ndevices, WORK_SET, ROW_WIDTH), work_acc.reshape(ndevices, WORK_SET))
    totals, deltas = lax.scan(device_grads, start, inputs)
    grad_up, grad_down, grad_bias = totals
    work_new = work_rows + deltas.reshape(-1, ROW_WIDTH)
    cache_split = cache_table.reshape(ndevices, CACHE_ROWS, ROW_WIDTH)
    hit_out = jax.vmap(masked_rows)(cache_split, hit_send.reshape(ndevices, N_PEER, HIT_CAP), hit_count.reshape(ndevices, N_PEER))
    hit_in = hit_out.reshape(N_GROUP, N_PEER, N_PEER, HIT_CAP, ROW_WIDTH).transpose(0, 2, 1, 3, 4).reshape(ndevices, N_PEER * HIT_CAP, ROW_WIDTH)
    home_split = home_table.reshape(ndevices, HOME_ROWS, ROW_WIDTH)
    miss_out = jax.vmap(masked_rows)(home_split, miss_send.reshape(ndevices, N_GROUP, MISS_CAP), miss_count.reshape(ndevices, N_GROUP))
    miss_in = miss_out.reshape(N_GROUP, N_PEER, N_GROUP, MISS_CAP, ROW_WIDTH).transpose(2, 1, 0, 3, 4).reshape(ndevices, N_GROUP * MISS_CAP, ROW_WIDTH)
    next_work = jnp.concatenate([hit_in, miss_in], axis=1).reshape(-1, ROW_WIDTH)
    evict_out = jax.vmap(masked_rows)(deltas, evict_slot.reshape(ndevices, N_GROUP, EVICT_CAP), evict_count.reshape(ndevices, N_GROUP))
    evict_in = evict_out.reshape(N_GROUP, N_PEER, N_GROUP, EVICT_CAP, ROW_WIDTH).transpose(2, 1, 0, 3, 4).reshape(ndevices, N_GROUP * EVICT_CAP, ROW_WIDTH)

    def add_home(home_block, dest_block, update_block):
        return home_block.at[dest_block.astype(jnp.int32)].add(update_block)
    home_new = jax.vmap(add_home)(home_split, evict_dest.reshape(ndevices, N_GROUP * EVICT_CAP), evict_in).reshape(-1, ROW_WIDTH)
    return (next_work, work_new, home_new, grad_up, grad_down, grad_bias)
```

```python
import jax
import jax.numpy as jnp
from jax import lax
from jax.experimental import pallas as pl
from jax.experimental.pallas import tpu as pltpu
from jax.sharding import PartitionSpec as P

MESH = pl.DeviceIdType.MESH
F32 = jnp.float32
BF16 = jnp.bfloat16

ROWW = 128
FEAT = 26
RANK = 256
BATCH = 384
WIDTH = 3456
SLOTS = 2048
HOME = 1024
CACHE = 512
HIT = 64
EVICT = 32
FOLD = 4
LINE = SLOTS // FOLD
NG = 16
NP = 16
STEP_SIZE = 0.5


def mm(a, b, dims=((1,), (0,))):
    return lax.dot_general(a, b, (dims, ((), ())), preferred_element_type=F32)


def tile_place(peer, t):
    part, tt = divmod(t, 7)
    return (peer // 8, peer % 8, part // 4, part % 4, tt)


def kernel(
    dense_h, upstream_h, ids_t, rows_h, acc_in, cache_h, home_h, up_h, down_h, bias_in, dest_in,
    hit_send, hit_count, miss_send, miss_count, evict_slot, evict_count,
    next_out, work_out, home_out, gup_out, gdown_out, gbias_out,
    stacked, upstream, gated, up, down, rows, cache, home, idb, folded, hidden, back, hidden_t,
    rg, delta, hit_buf, miss_buf, ev_buf, ev_in,
    grad, r0, ra1, a1, rb1, b1, rc1, c1, ra2, rb2, ab2, rc2, c2, rab, rc3, final, out_all,
    in_sem, hit_s, hit_r, miss_s, miss_r, ev_s, ev_r, core_s, core_r,
    a1_s, a1_r, b1_s, b1_r, c1_s, c1_r, a2_s, a2_r, b2_s, b2_r, c2_s, c2_r,
    z3_s, z3_r, c3_s, c3_r, ag_s, ag_r,
):
    g = lax.axis_index("group")
    p = lax.axis_index("peer")
    core = lax.rem(g, 2)
    x = lax.rem(g // 2, 4)
    yl = g // 8
    yh = p // 8
    z = lax.rem(p, 8)
    y = yh * 2 + yl

    def at_x(c):
        return ((yl * 4 + c) * 2 + core, p)

    def at_y(c):
        return ((lax.rem(c, 2) * 4 + x) * 2 + core, (c // 2) * 8 + z)

    def at_z(c):
        return (g, yh * 8 + c)

    loads = []
    for k, (src, dst) in enumerate((
        (cache_h, cache), (home_h, home), (rows_h, rows), (dense_h, stacked.at[:, 0:ROWW]),
        (upstream_h, upstream), (up_h, up), (down_h, down),
    )):
        c = pltpu.make_async_copy(src, dst, in_sem.at[k])
        c.start()
        loads.append(c)

    barrier = pltpu.get_barrier_semaphore()

    def greet(i, _):
        pl.semaphore_signal(barrier, inc=1, device_id=(lax.rem(g + i, NG), p), device_id_type=MESH)
        pl.semaphore_signal(barrier, inc=1, device_id=(g, lax.rem(p + i, NP)), device_id_type=MESH)
        return 0

    lax.fori_loop(1, 16, greet, 0)
    pl.semaphore_signal(
        barrier, inc=1, device_id=(((1 - yl) * 4 + x) * 2 + core, (1 - yh) * 8 + z), device_id_type=MESH
    )

    def pick(table, listed, counts, buf, many):
        def one(q, _):
            for k in range(many):
                buf[q, pl.ds(k, 1), :] = table[pl.ds(listed[q, k], 1), :]
            keep = lax.broadcasted_iota(jnp.int32, (many, ROWW), 0) < counts[q]
            buf[q] = jnp.where(keep, buf[q], 0.0)
            return 0

        lax.fori_loop(0, 16, one, 0)

    loads[0].wait()
    pick(cache, hit_send, hit_count, hit_buf, HIT)
    loads[1].wait()
    pick(home, miss_send, miss_count, miss_buf, HIT)
    pl.semaphore_wait(barrier, 31)

    def hit_copy(q, to):
        return pltpu.make_async_remote_copy(
            hit_buf.at[to], next_out.at[pl.ds(q * HIT, HIT), :], hit_s.at[to], hit_r.at[q],
            device_id=(g, to), device_id_type=MESH)

    def miss_copy(h, to):
        return pltpu.make_async_remote_copy(
            miss_buf.at[to], next_out.at[pl.ds(NP * HIT + h * HIT, HIT), :], miss_s.at[to], miss_r.at[h],
            device_id=(to, p), device_id_type=MESH)

    def send_rows(i, _):
        hit_copy(p, lax.rem(p + i, NP)).start()
        miss_copy(g, lax.rem(g + i, NG)).start()
        return 0

    lax.fori_loop(1, 16, send_rows, 0)
    next_out[pl.ds(p * HIT, HIT), :] = hit_buf[p]
    next_out[pl.ds(NP * HIT + g * HIT, HIT), :] = miss_buf[g]

    ids_n = jnp.concatenate([ids_t[...], jnp.zeros((ROWW - FEAT, BATCH), jnp.int32)], axis=0).T
    for f in range(FEAT):
        idb[f] = jnp.broadcast_to(ids_n[:, f:f + 1], (BATCH, ROWW))
    loads[2].wait()
    for j in range(FOLD):
        folded[:, j * ROWW:(j + 1) * ROWW] = rows[j * LINE:(j + 1) * LINE, :].astype(BF16)
    loads[3].wait()
    loads[4].wait()
    gated[:, 0:ROWW] = (upstream[:, 0:ROWW].astype(F32) * stacked[:, 0:ROWW].astype(F32)).astype(BF16)

    def look(f, _):
        ids = idb[f]
        low = ids & (LINE - 1)
        lane = lax.broadcasted_iota(jnp.int32, (BATCH, ROWW), 1)
        hot = jnp.concatenate(
            [jnp.where(low == lane + ROWW * j, 1.0, 0.0).astype(BF16) for j in range(LINE // ROWW)], axis=1)
        got = mm(hot, folded[...])
        high = ids >> 9
        row = got[:, 0:ROWW]
        for j in range(1, FOLD):
            row = jnp.where(high == j, got[:, j * ROWW:(j + 1) * ROWW], row)
        cols = pl.ds(pl.multiple_of((f + 1) * ROWW, ROWW), ROWW)
        stacked[:, cols] = row.astype(BF16)
        gated[:, cols] = (upstream[:, cols].astype(F32) * row).astype(BF16)
        return 0

    lax.fori_loop(0, FEAT, look, 0)

    loads[5].wait()
    hidden[...] = mm(stacked[...], up[...]).astype(BF16)
    loads[6].wait()
    back[...] = mm(gated[...], down[...], ((1,), (1,))).astype(BF16)
    hidden_t[0:RANK, :] = hidden[...].astype(F32).T.astype(BF16)
    hidden_t[RANK:, :] = jnp.ones((16, BATCH), BF16)

    sums = []
    for c0 in range(0, 27, 2):
        n = min(2, 27 - c0)
        cols = slice(c0 * ROWW, (c0 + n) * ROWW)
        d = mm(hidden_t[...], gated[:, cols])
        for c in range(n):
            for r in range(32):
                grad[(1,) + tile_place(r // 2, (r % 2) * 27 + c0 + c)] = d[8 * r:8 * r + 8, c * ROWW:(c + 1) * ROWW]
        sums.append(d[RANK:RANK + 8, :])
        u = mm(stacked[:, cols], back[...], ((0,), (0,)))
        for rr in range(16 * n):
            r = c0 * 16 + rr
            for c in range(2):
                grad[(0,) + tile_place(r // 27, (r % 27) * 2 + c)] = u[8 * rr:8 * rr + 8, c * ROWW:(c + 1) * ROWW]
    total = jnp.concatenate(sums + [jnp.zeros((8, 256), F32)], axis=1)
    first = lax.broadcasted_iota(jnp.int32, (8, ROWW), 0) == 0
    nil = jnp.zeros((8, ROWW), F32)
    for q in range(NP):
        start = (216 * q) // ROWW * ROWW
        piece = total[:, start:start + 384]
        if 216 * q > start:
            piece = pltpu.roll(piece, 384 - (216 * q - start), 1)
        grad[(0,) + tile_place(q, 54)] = jnp.where(first, piece[:, 0:ROWW], piece[:, ROWW:2 * ROWW])
        grad[(0,) + tile_place(q, 55)] = nil
        grad[(1,) + tile_place(q, 54)] = nil
        grad[(1,) + tile_place(q, 55)] = nil

    parts = ((6, 7), (0, 3), (3, 6))
    swaps = []
    for k, (lo, hi) in enumerate(parts):
        c = pltpu.make_async_remote_copy(
            grad.at[1 - core, :, :, :, :, lo:hi], r0.at[:, :, :, :, lo:hi], core_s.at[k], core_r.at[k],
            device_id=(g + 1 - 2 * core, p), device_id_type=MESH)
        c.start()
        swaps.append(c)

    def terms(i, _):
        cols = pl.ds(pl.multiple_of(ROWW + i * 256, ROWW), 256)
        cross = mm(hidden[...], down[:, cols])
        bias = bias_in[pl.ds(1 + 2 * i, 2), :]
        bias = jnp.concatenate([bias[0:1], bias[1:2]], axis=1)
        gi = upstream[:, cols].astype(F32) * (cross + bias + 1.0)
        gi = gi + mm(back[...], up[cols, :], ((1,), (1,)))
        for e in range(2):
            f = 2 * i + e
            term = gi[:, e * ROWW:(e + 1) * ROWW]
            high = idb[f] >> 9
            split = jnp.concatenate(
                [jnp.where(high == j, term, 0.0).astype(BF16) for j in range(FOLD)], axis=1)
            low = ids_t[pl.ds(f, 1), :] & (LINE - 1)
            hot = jnp.where(lax.broadcasted_iota(jnp.int32, (LINE, BATCH), 0) == low, 1.0, 0.0).astype(BF16)
            rg[...] += mm(hot, split)
        return 0

    rg[...] = jnp.zeros_like(rg)
    lax.fori_loop(0, 4, terms, 0)

    def ring4(me, dev, chunk, buf, ss, rs):
        right, left = lax.rem(me + 1, 4), lax.rem(me + 3, 4)
        far = lax.rem(me + 2, 4)

        def copy(src, slot, to):
            return pltpu.make_async_remote_copy(
                src, buf.at[slot], ss.at[slot], rs.at[slot], device_id=dev(to), device_id_type=MESH)

        copies = [
            copy(chunk(far, 0), 0, right), copy(chunk(far, 1), 1, left),
            copy(chunk(right, 1), 2, right), copy(chunk(left, 0), 3, left),
            copy(chunk(right, 0), 4, right), copy(chunk(left, 1), 5, left),
        ]

        def start():
            for c in copies[:4]:
                c.start()

        def middle():
            for s, piece in ((0, chunk(right, 0)), (1, chunk(left, 1))):
                copies[s].wait_recv()
                piece[...] = piece[...] + buf[s]
                copies[4 + s].start()

        def finish(put):
            for s in (2, 3, 4, 5):
                copies[s].wait_recv()
            put(0, chunk(me, 0)[...] + buf[3] + buf[4])
            put(1, chunk(me, 1)[...] + buf[2] + buf[5])

        def done():
            for c in copies:
                c.wait_send()

        return start, middle, finish, done

    def direct(n, me, dev, chunk, buf, ss, rs):
        copies = []
        for d in range(1, n):
            to = lax.rem(me + d, n)
            copies.append(pltpu.make_async_remote_copy(
                chunk(to), buf.at[d - 1], ss.at[d - 1], rs.at[d - 1], device_id=dev(to), device_id_type=MESH))

        def start():
            for c in copies:
                c.start()

        def finish():
            for c in copies:
                c.wait_recv()
            s = chunk(me)[...]
            for d in range(n - 1):
                s = s + buf[d]
            return s

        def done():
            for c in copies:
                c.wait_send()

        return start, finish, done

    xa = ring4(x, at_x, lambda c, h: r0.at[h, :, :, c, 0:3], ra1, a1_s, a1_r)
    yb = ring4(y, at_y, lambda c, h: r0.at[c // 2, 4 * h:4 * h + 4, lax.rem(c, 2), :, 3:6], rb1, b1_s, b1_r)
    zc = direct(8, z, at_z, lambda c: r0.at[:, c, :, :, 6], rc1, c1_s, c1_r)
    ya = ring4(y, at_y, lambda c, h: a1.at[c // 2, 4 * h:4 * h + 4, lax.rem(c, 2)], ra2, a2_s, a2_r)
    xb = ring4(x, at_x, lambda c, h: b1.at[4 * h:4 * h + 4, c], rb2, b2_s, b2_r)
    yc = direct(4, y, at_y, lambda c: c1.at[c // 2, lax.rem(c, 2)], rc2, c2_s, c2_r)
    zab = direct(8, z, at_z, lambda c: ab2.at[c], rab, z3_s, z3_r)
    xc = direct(4, x, at_x, lambda c: c2.at[c], rc3, c3_s, c3_r)

    def merge(k, begin):
        lo, hi = parts[k]
        swaps[k].wait_recv()

        def one(q, _):
            a, b = q // 8, lax.rem(q, 8)
            r0[a, b, :, :, lo:hi] = r0[a, b, :, :, lo:hi] + grad[core, a, b, :, :, lo:hi]
            return 0

        lax.fori_loop(0, 16, one, 0)
        begin()

    merge(0, zc[0])
    merge(1, xa[0])
    merge(2, yb[0])

    lax.fori_loop(4, 10, terms, 0)
    xa[1]()
    yb[1]()
    lax.fori_loop(10, 13, terms, 0)

    acc_t = jnp.concatenate([acc_in[...], jnp.zeros((112, ROWW), F32)], axis=0).T
    for b in range(16):
        j, i = divmod(b, 4)
        grads = rg[i * ROWW:(i + 1) * ROWW, j * ROWW:(j + 1) * ROWW]
        new = acc_t[:, b:b + 1] + jnp.mean(grads * grads, axis=1, keepdims=True)
        step = (-STEP_SIZE * grads) / jnp.sqrt(new)
        delta[b * ROWW:(b + 1) * ROWW, :] = step
        work_out[b * ROWW:(b + 1) * ROWW, :] = rows[b * ROWW:(b + 1) * ROWW, :] + step

    pick(delta, evict_slot, evict_count, ev_buf, EVICT)

    def ev_copy(src, to):
        return pltpu.make_async_remote_copy(
            ev_buf.at[to], ev_in.at[src], ev_s.at[to], ev_r.at[src], device_id=(to, p), device_id_type=MESH)

    def send_evicted(i, _):
        ev_copy(g, lax.rem(g + i, NG)).start()
        return 0

    lax.fori_loop(1, 16, send_evicted, 0)
    ev_in[g] = ev_buf[g]

    def put_c1(v):
        c1[...] = v

    put_c1(zc[1]())
    yc[0]()

    def put_a1(h, v):
        a1[h] = v

    xa[2](put_a1)
    ya[0]()

    def put_b1(h, v):
        b1[4 * h:4 * h + 4] = v

    yb[2](put_b1)
    xb[0]()
    c2[...] = yc[1]()
    xc[0]()
    ya[1]()
    xb[1]()

    def put_a2(h, v):
        ab2[4 * h:4 * h + 4, 0:3] = v

    def put_b2(h, v):
        ab2[4 * h:4 * h + 4, 3:6] = v

    ya[2](put_a2)
    xb[2](put_b2)
    zab[0]()

    def got_evicted(i, _):
        ev_copy(lax.rem(g + i, NG), lax.rem(g + i, NG)).wait_recv()
        return 0

    lax.fori_loop(1, 16, got_evicted, 0)
    place = jnp.concatenate([dest_in[k:k + 1, :] for k in range(4)], axis=1)
    hot = jnp.where(lax.broadcasted_iota(jnp.int32, (HOME, NG * EVICT), 0) == place, 1.0, 0.0).astype(BF16)
    home_out[...] = home[...] + mm(hot, ev_in[...].reshape(NG * EVICT, ROWW).astype(BF16))

    final[6] = xc[1]()
    final[0:6] = zab[1]()

    def ag_copy(src, to):
        return pltpu.make_async_remote_copy(
            final, out_all.at[lax.rem(src, 2), src // 8, lax.rem(src // 2, 4)], ag_s.at[to], ag_r.at[src],
            device_id=(to, p), device_id_type=MESH)

    def spread(i, _):
        ag_copy(g, lax.rem(g + i, NG)).start()
        return 0

    lax.fori_loop(1, 16, spread, 0)
    out_all[core, yl, x] = final[...]

    def got_rows(i, _):
        q = lax.rem(p + i, NP)
        h = lax.rem(g + i, NG)
        hit_copy(q, q).wait_recv()
        miss_copy(h, h).wait_recv()
        hit_copy(q, q).wait_send()
        miss_copy(h, h).wait_send()
        ev_copy(h, h).wait_send()
        return 0

    lax.fori_loop(1, 16, got_rows, 0)
    for c in swaps:
        c.wait_send()
    for phase in (xa, yb, zc, ya, xb, yc, zab, xc):
        phase[-1]()

    def got_all(i, _):
        h = lax.rem(g + i, NG)
        ag_copy(h, h).wait()
        return 0

    lax.fori_loop(1, 16, got_all, 0)

    def tile(c, t):
        part, tt = divmod(t, 7)
        return out_all[c, part // 4, part % 4, tt]

    for r in range(27):
        for c in range(2):
            gup_out[8 * r:8 * r + 8, c * ROWW:(c + 1) * ROWW] = tile(0, 2 * r + c)
    for r in range(2):
        for c in range(27):
            gdown_out[8 * r:8 * r + 8, c * ROWW:(c + 1) * ROWW] = tile(1, 27 * r + c)
    gbias_out[...] = tile(0, 54)


def body(
    dense_feat, upstream, cur_ids, work_rows, work_acc, cache_table, home_table, hit_send, hit_count,
    miss_send, miss_count, evict_slot, evict_dest, evict_count, up_proj, down_proj, cross_bias,
):
    vmem = pl.BlockSpec(memory_space=pltpu.VMEM)
    smem = pl.BlockSpec(memory_space=pltpu.SMEM)
    anyw = pl.BlockSpec(memory_space=pl.ANY)
    dma = pltpu.SemaphoreType.DMA
    v = pltpu.VMEM
    t = (8, 128)
    scratch = [
        v((BATCH, WIDTH), BF16), v((BATCH, WIDTH), BF16), v((BATCH, WIDTH), BF16),
        v((WIDTH, RANK), BF16), v((RANK, WIDTH), BF16), v((SLOTS, ROWW), F32), v((CACHE, ROWW), F32),
        v((HOME, ROWW), F32), v((FEAT, BATCH, ROWW), jnp.int32), v((LINE, FOLD * ROWW), BF16),
        v((BATCH, RANK), BF16), v((BATCH, RANK), BF16), v((RANK + 16, BATCH), BF16),
        v((LINE, FOLD * ROWW), F32), v((SLOTS, ROWW), F32),
        v((NP, HIT, ROWW), F32), v((NG, HIT, ROWW), F32), v((NG, EVICT, ROWW), F32), v((NG, EVICT, ROWW), F32),
        v((2, 2, 8, 2, 4, 7) + t, F32), v((2, 8, 2, 4, 7) + t, F32),
        v((6, 8, 2, 3) + t, F32), v((2, 8, 2, 3) + t, F32),
        v((6, 4, 4, 3) + t, F32), v((8, 4, 3) + t, F32),
        v((7, 2, 2, 4) + t, F32), v((2, 2, 4) + t, F32),
        v((6, 4, 3) + t, F32), v((6, 4, 3) + t, F32), v((8, 6) + t, F32),
        v((3, 4) + t, F32), v((4,) + t, F32), v((7, 6) + t, F32), v((3,) + t, F32),
        v((7,) + t, F32), v((2, 2, 4, 7) + t, F32),
        dma((7,)), dma((16,)), dma((16,)), dma((16,)), dma((16,)), dma((16,)), dma((16,)), dma((3,)), dma((3,)),
        dma((6,)), dma((6,)), dma((6,)), dma((6,)), dma((7,)), dma((7,)),
        dma((6,)), dma((6,)), dma((6,)), dma((6,)), dma((3,)), dma((3,)),
        dma((7,)), dma((7,)), dma((3,)), dma((3,)), dma((16,)), dma((16,)),
    ]
    out = pl.pallas_call(
        kernel,
        out_shape=(
            jax.ShapeDtypeStruct((SLOTS, ROWW), F32),
            jax.ShapeDtypeStruct((SLOTS, ROWW), F32),
            jax.ShapeDtypeStruct((HOME, ROWW), F32),
            jax.ShapeDtypeStruct((216, RANK), F32),
            jax.ShapeDtypeStruct((16, WIDTH), F32),
            jax.ShapeDtypeStruct((8, ROWW), F32),
        ),
        in_specs=[anyw, anyw, vmem, anyw, vmem, anyw, anyw, anyw, anyw, vmem, vmem] + [smem] * 6,
        out_specs=(vmem,) * 6,
        scratch_shapes=scratch,
        compiler_params=pltpu.CompilerParams(
            collective_id=0, has_side_effects=True, vmem_limit_bytes=60 * 1024 * 1024),
        name="cross_step",
    )(
        dense_feat, upstream, cur_ids.T, work_rows, work_acc.reshape(16, ROWW), cache_table, home_table,
        up_proj, down_proj, cross_bias.reshape(27, ROWW), evict_dest.reshape(4, ROWW),
        hit_send, hit_count, miss_send, miss_count, evict_slot, evict_count,
    )
    next_work, work_new, home_new, grad_up, grad_down, grad_bias = out
    return next_work, work_new, home_new, grad_up, grad_down, grad_bias.reshape(-1)[:216]


def solution(mesh):
    rows = P(("group", "peer"), None)
    flat = P(("group", "peer"))
    return jax.shard_map(
        body,
        mesh=mesh,
        in_specs=(rows, rows, rows, rows, flat, rows, rows, rows, flat, rows, flat, rows, rows, flat, P(), P(), P()),
        out_specs=(rows, rows, rows, P("peer", None), P("peer", None), P("peer")),
        check_vma=False,
    )
```

```python
import jax
import jax.numpy as jnp
from jax import lax
from jax.experimental import pallas as pl
from jax.experimental.pallas import tpu as pltpu
from jax.sharding import PartitionSpec as P

MESH = pl.DeviceIdType.MESH
F32 = jnp.float32
BF16 = jnp.bfloat16

ROWW = 128
FEAT = 26
RANK = 256
BATCH = 384
WIDTH = 3456
SLOTS = 2048
HOME = 1024
CACHE = 512
HIT = 64
EVICT = 32
FOLD = 4
LINE = SLOTS // FOLD
NG = 16
NP = 16
STEP_SIZE = 0.5


def mm(a, b, dims=((1,), (0,))):
    return lax.dot_general(a, b, (dims, ((), ())), preferred_element_type=F32)


def tile_place(peer, t):
    part, tt = divmod(t, 7)
    return (peer // 8, peer % 8, part // 4, part % 4, tt)


WAVES = (((0, 2), (2, 4)), ((5, 6), (6, 7)))
Z_TILE = 4
FIRST = 5
T = (8, 128)


def scratch_list():
    v = pltpu.VMEM
    dma = pltpu.SemaphoreType.DMA
    items = [
        ("stacked", v((BATCH, WIDTH), BF16)), ("upstream", v((BATCH, WIDTH), BF16)), ("gated", v((BATCH, WIDTH), BF16)),
        ("up", v((WIDTH, RANK), BF16)), ("down", v((RANK, WIDTH), BF16)), ("rows", v((SLOTS, ROWW), F32)),
        ("cache", v((CACHE, ROWW), F32)), ("home", v((HOME, ROWW), F32)), ("ids_n", v((BATCH, ROWW), jnp.int32)),
        ("idb", v((FEAT, BATCH, ROWW), jnp.int32)), ("folded", v((LINE, FOLD * ROWW), BF16)),
        ("hidden", v((BATCH, RANK), BF16)), ("back", v((BATCH, RANK), BF16)), ("hidden_t", v((RANK + 16, BATCH), BF16)),
        ("rg", v((LINE, FOLD * ROWW), F32)), ("delta", v((SLOTS, ROWW), F32)),
        ("hit_buf", v((NP, HIT, ROWW), F32)), ("miss_buf", v((NG, HIT, ROWW), F32)),
        ("ev_buf", v((NG, EVICT, ROWW), F32)), ("ev_in", v((NG, EVICT, ROWW), F32)),
        ("grad", v((2, 2, 8, 2, 4, 7) + T, F32)), ("r0", v((2, 8, 2, 4, 7) + T, F32)),
        ("rc1", v((7, 2, 2, 4) + T, F32)), ("c1", v((2, 2, 4) + T, F32)), ("rc2", v((3, 4) + T, F32)),
        ("c2", v((4,) + T, F32)), ("rc3", v((3,) + T, F32)),
        ("final", v((7,) + T, F32)), ("out_all", v((2, 2, 4, 7) + T, F32)),
        ("ag_like", v((NG - 1, 7) + T, F32)), ("in_sem", dma((7,))), ("out_sem", dma((2,))), ("core_s", dma((1,))), ("core_r", dma((5,))),
    ]
    for name in ("hit", "miss", "ev", "ag0", "ag1"):
        items += [(name + "_s", dma((1,))), (name + "_r", dma((1,)))]
    for name in ("c1", "c2", "c3"):
        items += [(name + "_s", dma((1,))), (name + "_r", dma((1,)))]
    for w, ((lo, hi), _) in enumerate(WAVES):
        n = hi - lo
        k = str(w)
        items += [
            ("ra1" + k, v((6, 8, 2, n) + T, F32)), ("a1" + k, v((2, 8, 2, n) + T, F32)),
            ("rb1" + k, v((6, 4, 4, n) + T, F32)), ("b1" + k, v((8, 4, n) + T, F32)),
            ("ra2" + k, v((6, 4, n) + T, F32)), ("rb2" + k, v((6, 4, n) + T, F32)),
            ("ab" + k, v((8, 2 * n) + T, F32)), ("rab" + k, v((7, 2 * n) + T, F32)),
        ]
        for name, m in (("xa", 3), ("yb", 3), ("ya", 3), ("xb", 3), ("z", 1)):
            items += [(name + k + "_s", dma((1,))), (name + k + "_r", dma((m,)))]
    return items


class Bag:
    pass


def kernel(*refs):
    names = [
        "dense_h", "upstream_h", "ids_t", "rows_h", "acc_in", "cache_h", "home_h", "up_h", "down_h", "bias_in", "dest_in",
        "hit_send", "hit_count", "miss_send", "miss_count", "evict_slot", "evict_count",
        "next_out", "work_out", "home_out", "gup_out", "gdown_out", "gbias_out",
    ] + [name for name, _ in scratch_list()]
    b = Bag()
    for name, ref in zip(names, refs, strict=True):
        setattr(b, name, ref)
    stacked, upstream, gated, idb, rg = b.stacked, b.upstream, b.gated, b.idb, b.rg

    g = lax.axis_index("group")
    p = lax.axis_index("peer")
    core = lax.rem(g, 2)
    x = lax.rem(g // 2, 4)
    yl = g // 8
    yh = p // 8
    z = lax.rem(p, 8)
    y = yh * 2 + yl

    def at_x(c):
        return ((yl * 4 + c) * 2 + core, p)

    def at_y(c):
        return ((lax.rem(c, 2) * 4 + x) * 2 + core, (c // 2) * 8 + z)

    def at_z(c):
        return (g, yh * 8 + c)

    loads = []
    for k, (src, dst) in enumerate((
        (b.rows_h, b.rows), (b.dense_h, stacked.at[:, 0:ROWW]), (b.upstream_h, upstream),
        (b.cache_h, b.cache), (b.home_h, b.home), (b.up_h, b.up), (b.down_h, b.down),
    )):
        c = pltpu.make_async_copy(src, dst, b.in_sem.at[k])
        c.start()
        loads.append(c)

    barrier = pltpu.get_barrier_semaphore()

    def greet(i, _):
        pl.semaphore_signal(barrier, inc=1, device_id=(lax.rem(g + i, NG), p), device_id_type=MESH)
        pl.semaphore_signal(barrier, inc=1, device_id=(g, lax.rem(p + i, NP)), device_id_type=MESH)
        return 0

    lax.fori_loop(1, 16, greet, 0)
    pl.semaphore_signal(
        barrier, inc=1, device_id=(((1 - yl) * 4 + x) * 2 + core, (1 - yh) * 8 + z), device_id_type=MESH
    )

    def pick(q, table, listed, counts, buf, many):
        for k in range(many):
            buf[q, pl.ds(k, 1), :] = table[pl.ds(listed[q, k], 1), :]
        keep = lax.broadcasted_iota(jnp.int32, (many, ROWW), 0) < counts[q]
        buf[q] = jnp.where(keep, buf[q], 0.0)

    def hit_copy(q, to):
        return pltpu.make_async_remote_copy(
            b.hit_buf.at[to], b.next_out.at[pl.ds(q * HIT, HIT), :], b.hit_s.at[0], b.hit_r.at[0],
            device_id=(g, to), device_id_type=MESH)

    def miss_copy(h, to):
        return pltpu.make_async_remote_copy(
            b.miss_buf.at[to], b.next_out.at[pl.ds(NP * HIT + h * HIT, HIT), :], b.miss_s.at[0], b.miss_r.at[0],
            device_id=(to, p), device_id_type=MESH)

    b.ids_n[...] = jnp.concatenate([b.ids_t[...], jnp.zeros((ROWW - FEAT, BATCH), jnp.int32)], axis=0).T
    loads[0].wait()
    for j in range(FOLD):
        b.folded[:, j * ROWW:(j + 1) * ROWW] = b.rows[j * LINE:(j + 1) * LINE, :].astype(BF16)
    loads[1].wait()
    loads[2].wait()
    gated[:, 0:ROWW] = (upstream[:, 0:ROWW].astype(F32) * stacked[:, 0:ROWW].astype(F32)).astype(BF16)
    loads[3].wait()
    loads[4].wait()

    def look(i):
        turned = pltpu.roll(b.ids_n[...], lax.rem(ROWW - 2 * i, ROWW), 1)
        lane = lax.broadcasted_iota(jnp.int32, (BATCH, ROWW), 1)
        hots = []
        for e in range(2):
            ids = jnp.broadcast_to(turned[:, e:e + 1], (BATCH, ROWW))
            idb[2 * i + e] = ids
            low = ids & (LINE - 1)
            hots.append(jnp.concatenate(
                [jnp.where(low == lane + ROWW * j, 1.0, 0.0).astype(BF16) for j in range(LINE // ROWW)], axis=1))
        got = mm(jnp.concatenate(hots, axis=0), b.folded[...])
        for e in range(2):
            high = idb[2 * i + e] >> 9
            part = got[e * BATCH:(e + 1) * BATCH]
            row = part[:, 0:ROWW]
            for j in range(1, FOLD):
                row = jnp.where(high == j, part[:, j * ROWW:(j + 1) * ROWW], row)
            cols = pl.ds(pl.multiple_of((2 * i + e + 1) * ROWW, ROWW), ROWW)
            stacked[:, cols] = row.astype(BF16)
            gated[:, cols] = (upstream[:, cols].astype(F32) * row).astype(BF16)

    def look_pick(i, _):
        offs = [2 * i + 1, 2 * i + 2]
        for o in offs:
            pick(lax.rem(p + o, NP), b.cache, b.hit_send, b.hit_count, b.hit_buf, HIT)
            pick(lax.rem(g + o, NG), b.home, b.miss_send, b.miss_count, b.miss_buf, HIT)
        look(i)
        for o in offs:
            @pl.when(o < 16)
            def _():
                hit_copy(p, lax.rem(p + o, NP)).start()
                miss_copy(g, lax.rem(g + o, NG)).start()
        return 0

    def look_only(i, _):
        look(i)
        return 0

    pl.semaphore_wait(barrier, 31)
    lax.fori_loop(0, 8, look_pick, 0)
    own_hit = pltpu.make_async_copy(b.hit_buf.at[p], b.next_out.at[pl.ds(p * HIT, HIT), :], b.out_sem.at[0])
    own_miss = pltpu.make_async_copy(
        b.miss_buf.at[g], b.next_out.at[pl.ds(NP * HIT + g * HIT, HIT), :], b.out_sem.at[1])
    own_hit.start()
    own_miss.start()
    lax.fori_loop(8, 13, look_only, 0)

    loads[5].wait()
    b.hidden[...] = mm(stacked[...], b.up[...]).astype(BF16)
    loads[6].wait()
    b.back[...] = mm(gated[...], b.down[...], ((1,), (1,))).astype(BF16)
    b.hidden_t[0:RANK, :] = b.hidden[...].astype(F32).T.astype(BF16)
    b.hidden_t[RANK:, :] = jnp.ones((16, BATCH), BF16)

    sums = []
    grad = b.grad
    for c0 in range(0, 27, 2):
        n = min(2, 27 - c0)
        cols = slice(c0 * ROWW, (c0 + n) * ROWW)
        d = mm(b.hidden_t[...], gated[:, cols])
        for c in range(n):
            for r in range(32):
                grad[(1,) + tile_place(r // 2, (r % 2) * 27 + c0 + c)] = d[8 * r:8 * r + 8, c * ROWW:(c + 1) * ROWW]
        sums.append(d[RANK:RANK + 8, :])
        u = mm(stacked[:, cols], b.back[...], ((0,), (0,)))
        for rr in range(16 * n):
            r = c0 * 16 + rr
            for c in range(2):
                grad[(0,) + tile_place(r // 27, (r % 27) * 2 + c)] = u[8 * rr:8 * rr + 8, c * ROWW:(c + 1) * ROWW]
    total = jnp.concatenate(sums + [jnp.zeros((8, 256), F32)], axis=1)
    first = lax.broadcasted_iota(jnp.int32, (8, ROWW), 0) == 0
    nil = jnp.zeros((8, ROWW), F32)
    for q in range(NP):
        start = (216 * q) // ROWW * ROWW
        piece = total[:, start:start + 384]
        if 216 * q > start:
            piece = pltpu.roll(piece, 384 - (216 * q - start), 1)
        grad[(0,) + tile_place(q, 54)] = jnp.where(first, piece[:, 0:ROWW], piece[:, ROWW:2 * ROWW])
        grad[(0,) + tile_place(q, 55)] = nil
        grad[(1,) + tile_place(q, 54)] = nil
        grad[(1,) + tile_place(q, 55)] = nil

    r0 = b.r0
    parts = ((Z_TILE, Z_TILE + 1),) + WAVES[0] + WAVES[1]
    swaps = []
    for k, (lo, hi) in enumerate(parts):
        c = pltpu.make_async_remote_copy(
            grad.at[1 - core, :, :, :, :, lo:hi], r0.at[:, :, :, :, lo:hi], b.core_s.at[0], b.core_r.at[k],
            device_id=(g + 1 - 2 * core, p), device_id_type=MESH)
        c.start()
        swaps.append(c)

    def merge(k):
        lo, hi = parts[k]
        swaps[k].wait_recv()

        def one(q, _):
            i, j = q // 8, lax.rem(q, 8)
            r0[i, j, :, :, lo:hi] = r0[i, j, :, :, lo:hi] + grad[core, i, j, :, :, lo:hi]
            return 0

        lax.fori_loop(0, 16, one, 0)

    def terms(i, _):
        cols = pl.ds(pl.multiple_of(ROWW + i * 256, ROWW), 256)
        cross = mm(b.hidden[...], b.down[:, cols])
        bias = b.bias_in[pl.ds(1 + 2 * i, 2), :]
        bias = jnp.concatenate([bias[0:1], bias[1:2]], axis=1)
        gi = upstream[:, cols].astype(F32) * (cross + bias + 1.0)
        gi = gi + mm(b.back[...], b.up[cols, :], ((1,), (1,)))
        for e in range(2):
            f = 2 * i + e
            term = gi[:, e * ROWW:(e + 1) * ROWW]
            high = idb[f] >> 9
            split = jnp.concatenate(
                [jnp.where(high == j, term, 0.0).astype(BF16) for j in range(FOLD)], axis=1)
            low = b.ids_t[pl.ds(f, 1), :] & (LINE - 1)
            hot = jnp.where(lax.broadcasted_iota(jnp.int32, (LINE, BATCH), 0) == low, 1.0, 0.0).astype(BF16)
            rg[...] += mm(hot, split)
        return 0

    def await_bytes(ref, sem):
        pltpu.make_async_copy(ref, ref, sem).wait()

    def ring4(me, dev, chunk, buf, ss, rs, put):
        right, left = lax.rem(me + 1, 4), lax.rem(me + 3, 4)
        far = lax.rem(me + 2, 4)

        def copy(src, slot, to):
            return pltpu.make_async_remote_copy(
                src, buf.at[slot], ss.at[0], rs.at[min(slot, 2)], device_id=dev(to), device_id_type=MESH)

        copies = [
            copy(chunk(far, 0), 0, right), copy(chunk(far, 1), 1, left),
            copy(chunk(right, 1), 2, right), copy(chunk(left, 0), 3, left),
            copy(chunk(right, 0), 4, right), copy(chunk(left, 1), 5, left),
        ]

        def start():
            for c in copies[:4]:
                c.start()

        def middle():
            for s, piece in ((0, chunk(right, 0)), (1, chunk(left, 1))):
                copies[s].wait_recv()
                piece[...] = piece[...] + buf[s]
                copies[4 + s].start()

        def finish():
            await_bytes(buf.at[2:6], rs.at[2])
            put(0, chunk(me, 0)[...] + buf[3] + buf[4])
            put(1, chunk(me, 1)[...] + buf[2] + buf[5])

        def done():
            await_bytes(buf, ss.at[0])

        return start, middle, finish, done

    def direct(n, me, dev, chunk, buf, ss, rs, put):
        copies = []
        for d in range(1, n):
            to = lax.rem(me + d, n)
            copies.append(pltpu.make_async_remote_copy(
                chunk(to), buf.at[d - 1], ss.at[0], rs.at[0], device_id=dev(to), device_id_type=MESH))

        def start():
            for c in copies:
                c.start()

        def finish():
            await_bytes(buf, rs.at[0])
            s = chunk(me)[...]
            for d in range(n - 1):
                s = s + buf[d]
            put(s)

        def done():
            await_bytes(buf, ss.at[0])

        return start, finish, done

    def setter(ref, at):
        def put(*v):
            ref[at(*v[:-1])] = v[-1]
        return put

    def sl(lo, hi):
        return slice(lo, hi)

    xa, yb, ya, xb, zw = [], [], [], [], []
    for w, ((alo, ahi), (blo, bhi)) in enumerate(WAVES):
        k = str(w)
        n = ahi - alo
        t = {m: getattr(b, m + k) for m in (
            "ra1", "a1", "rb1", "b1", "ra2", "rb2", "ab", "rab", "xa", "yb", "ya", "xb", "z") if hasattr(b, m + k)}
        sems = {m: (getattr(b, m + k + "_s"), getattr(b, m + k + "_r")) for m in ("xa", "yb", "ya", "xb", "z")}
        xa.append(ring4(
            x, at_x, lambda c, h, lo=alo, hi=ahi: r0.at[h, :, :, c, lo:hi], t["ra1"], *sems["xa"],
            setter(t["a1"], lambda h: h)))
        yb.append(ring4(
            y, at_y, lambda c, h, lo=blo, hi=bhi: r0.at[c // 2, 4 * h:4 * h + 4, lax.rem(c, 2), :, lo:hi],
            t["rb1"], *sems["yb"], setter(t["b1"], lambda h: sl(4 * h, 4 * h + 4))))
        ya.append(ring4(
            y, at_y, lambda c, h, r=t["a1"]: r.at[c // 2, 4 * h:4 * h + 4, lax.rem(c, 2)], t["ra2"], *sems["ya"],
            setter(t["ab"], lambda h, n=n: (sl(4 * h, 4 * h + 4), sl(0, n)))))
        xb.append(ring4(
            x, at_x, lambda c, h, r=t["b1"]: r.at[4 * h:4 * h + 4, c], t["rb2"], *sems["xb"],
            setter(t["ab"], lambda h, n=n: (sl(4 * h, 4 * h + 4), sl(n, 2 * n)))))
        zw.append(direct(
            8, z, at_z, lambda c, r=t["ab"]: r.at[c], t["rab"], *sems["z"],
            setter(b.final, lambda lo=alo, hi=bhi: sl(lo, hi))))
    zc = direct(
        8, z, at_z, lambda c: r0.at[:, c, :, :, Z_TILE], b.rc1, b.c1_s, b.c1_r, setter(b.c1, lambda: Ellipsis))
    yc = direct(
        4, y, at_y, lambda c: b.c1.at[c // 2, lax.rem(c, 2)], b.rc2, b.c2_s, b.c2_r, setter(b.c2, lambda: Ellipsis))
    xc = direct(4, x, at_x, lambda c: b.c2.at[c], b.rc3, b.c3_s, b.c3_r, setter(b.final, lambda: Z_TILE))

    def ev_copy(src, to):
        return pltpu.make_async_remote_copy(
            b.ev_buf.at[to], b.ev_in.at[src], b.ev_s.at[0], b.ev_r.at[0], device_id=(to, p), device_id_type=MESH)

    def adagrad():
        acc_t = jnp.concatenate([b.acc_in[...], jnp.zeros((112, ROWW), F32)], axis=0).T
        for k in range(16):
            j, i = divmod(k, 4)
            grads = rg[i * ROWW:(i + 1) * ROWW, j * ROWW:(j + 1) * ROWW]
            new = acc_t[:, k:k + 1] + jnp.mean(grads * grads, axis=1, keepdims=True)
            step = (-STEP_SIZE * grads) / jnp.sqrt(new)
            b.delta[k * ROWW:(k + 1) * ROWW, :] = step
            b.work_out[k * ROWW:(k + 1) * ROWW, :] = b.rows[k * ROWW:(k + 1) * ROWW, :] + step

    def evict():
        def one(i, _):
            pick(lax.rem(g + i, NG), b.delta, b.evict_slot, b.evict_count, b.ev_buf, EVICT)

            @pl.when(i < 16)
            def _():
                ev_copy(g, lax.rem(g + i, NG)).start()
            return 0

        lax.fori_loop(1, 17, one, 0)
        b.ev_in[g] = b.ev_buf[g]

    def settle_home():
        await_bytes(b.ev_in.at[0:NG - 1], b.ev_r.at[0])
        place = jnp.concatenate([b.dest_in[k:k + 1, :] for k in range(NG)], axis=1)
        hot = jnp.where(lax.broadcasted_iota(jnp.int32, (HOME, NG * EVICT), 0) == place, 1.0, 0.0).astype(BF16)
        b.home_out[...] = b.home[...] + mm(hot, b.ev_in[...].reshape(NG * EVICT, ROWW).astype(BF16))

    def ag_copy(w, src, to):
        lo, hi = ((0, FIRST), (FIRST, 7))[w]
        ss, rs = ((b.ag0_s, b.ag0_r), (b.ag1_s, b.ag1_r))[w]
        return pltpu.make_async_remote_copy(
            b.final.at[lo:hi], b.out_all.at[lax.rem(src, 2), src // 8, lax.rem(src // 2, 4), lo:hi],
            ss.at[0], rs.at[0], device_id=(to, p), device_id_type=MESH)

    def spread(w):
        def one(i, _):
            ag_copy(w, g, lax.rem(g + i, NG)).start()
            return 0

        lax.fori_loop(1, 16, one, 0)
        lo, hi = ((0, FIRST), (FIRST, 7))[w]
        b.out_all[core, yl, x, lo:hi] = b.final[lo:hi]

    def run_terms(lo, hi):
        lax.fori_loop(lo, hi, terms, 0)

    rg[...] = jnp.zeros_like(rg)
    run_terms(0, 1)
    merge(0)
    zc[0]()
    run_terms(1, 2)
    merge(1)
    xa[0][0]()
    merge(2)
    yb[0][0]()
    merge(3)
    merge(4)
    run_terms(2, 6)
    xa[0][1]()
    xa[1][0]()
    yb[0][1]()
    yb[1][0]()
    run_terms(6, 10)
    xa[0][2]()
    ya[0][0]()
    xa[1][1]()
    yb[0][2]()
    xb[0][0]()
    yb[1][1]()
    run_terms(10, 13)
    xa[1][2]()
    ya[1][0]()
    yb[1][2]()
    xb[1][0]()
    ya[0][1]()
    xb[0][1]()
    zc[1]()
    yc[0]()
    adagrad()
    ya[1][1]()
    xb[1][1]()
    ya[0][2]()
    xb[0][2]()
    zw[0][0]()
    evict()
    yc[1]()
    xc[0]()
    ya[1][2]()
    xb[1][2]()
    zw[1][0]()
    xc[1]()
    zw[0][1]()
    spread(0)
    settle_home()
    zw[1][1]()
    spread(1)

    for sems in ((b.hit_s, b.hit_r), (b.miss_s, b.miss_r)):
        for sem in sems:
            await_bytes(b.hit_buf.at[0:NP - 1], sem.at[0])
    await_bytes(b.ev_buf.at[0:NG - 1], b.ev_s.at[0])
    await_bytes(r0, b.core_s.at[0])
    for phase in xa + yb + ya + xb + zw + [zc, yc, xc]:
        phase[-1]()
    own_hit.wait()
    own_miss.wait()
    for (lo, hi), sems in (((0, FIRST), (b.ag0_s, b.ag0_r)), ((FIRST, 7), (b.ag1_s, b.ag1_r))):
        for sem in sems:
            await_bytes(b.ag_like.at[:, lo:hi], sem.at[0])

    def tile(c, t):
        part, tt = divmod(t, 7)
        return b.out_all[c, part // 4, part % 4, tt]

    for r in range(27):
        for c in range(2):
            b.gup_out[8 * r:8 * r + 8, c * ROWW:(c + 1) * ROWW] = tile(0, 2 * r + c)
    for r in range(2):
        for c in range(27):
            b.gdown_out[8 * r:8 * r + 8, c * ROWW:(c + 1) * ROWW] = tile(1, 27 * r + c)
    b.gbias_out[...] = tile(0, 54)


def hand_on(n_in, w_in, h_in, u_in, d_in, b_in, n_out, w_out, h_out, u_out, d_out, b_out, sems):
    copies = []
    for k, (src, dst) in enumerate(zip((n_in, w_in, h_in, u_in, d_in), (n_out, w_out, h_out, u_out, d_out))):
        c = pltpu.make_async_copy(src, dst, sems.at[k])
        c.start()
        copies.append(c)
    b_out[0:ROWW] = b_in[0]
    b_out[ROWW:216] = b_in[1, 0:216 - ROWW]
    for c in copies:
        c.wait()


def body(
    dense_feat, upstream, cur_ids, work_rows, work_acc, cache_table, home_table, hit_send, hit_count,
    miss_send, miss_count, evict_slot, evict_dest, evict_count, up_proj, down_proj, cross_bias,
):
    vmem = pl.BlockSpec(memory_space=pltpu.VMEM)
    smem = pl.BlockSpec(memory_space=pltpu.SMEM)
    anyw = pl.BlockSpec(memory_space=pl.ANY)
    shapes = [
        jax.ShapeDtypeStruct(s, F32)
        for s in ((SLOTS, ROWW), (SLOTS, ROWW), (HOME, ROWW), (216, RANK), (16, WIDTH), (8, ROWW))
    ]
    out = pl.pallas_call(
        kernel,
        out_shape=tuple(pltpu.VMEM(s.shape, F32) for s in shapes),
        in_specs=[anyw, anyw, vmem, anyw, vmem, anyw, anyw, anyw, anyw, vmem, vmem] + [smem] * 6,
        out_specs=(vmem,) * 6,
        scratch_shapes=[s for _, s in scratch_list()],
        compiler_params=pltpu.CompilerParams(
            collective_id=0, has_side_effects=True, vmem_limit_bytes=60 * 1024 * 1024),
        name="cross_step",
    )(
        dense_feat, upstream, cur_ids.T, work_rows, work_acc.reshape(16, ROWW), cache_table, home_table,
        up_proj, down_proj, cross_bias.reshape(27, ROWW), evict_dest,
        hit_send, hit_count, miss_send, miss_count, evict_slot, evict_count,
    )
    return pl.pallas_call(
        hand_on,
        out_shape=tuple(shapes[:5]) + (jax.ShapeDtypeStruct((216,), F32),),
        in_specs=[vmem] * 6,
        out_specs=(anyw,) * 5 + (vmem,),
        scratch_shapes=[pltpu.SemaphoreType.DMA((5,))],
        compiler_params=pltpu.CompilerParams(vmem_limit_bytes=4 * 1024 * 1024),
        name="hand_on",
    )(*[pltpu.with_memory_space_constraint(o, pltpu.VMEM) for o in out])


def solution(mesh):
    rows = P(("group", "peer"), None)
    flat = P(("group", "peer"))
    return jax.shard_map(
        body,
        mesh=mesh,
        in_specs=(rows, rows, rows, rows, flat, rows, rows, rows, flat, rows, flat, rows, rows, flat, P(), P(), P()),
        out_specs=(rows, rows, rows, P("peer", None), P("peer", None), P("peer")),
        check_vma=False,
    )
```

```python
import jax
import jax.numpy as jnp
from jax import lax
from jax.experimental import pallas as pl
from jax.experimental.pallas import tpu as pltpu
from jax.sharding import PartitionSpec as P

MESH = pl.DeviceIdType.MESH
F32 = jnp.float32
BF16 = jnp.bfloat16

ROWW = 128
FEAT = 26
RANK = 256
BATCH = 384
WIDTH = 3456
SLOTS = 2048
HOME = 1024
CACHE = 512
HIT = 64
EVICT = 32
FOLD = 4
LINE = SLOTS // FOLD
NG = 16
NP = 16
STEP_SIZE = 0.5


def mm(a, b, dims=((1,), (0,))):
    return lax.dot_general(a, b, (dims, ((), ())), preferred_element_type=F32)


def tile_place(peer, t):
    part, tt = divmod(t, 7)
    return (peer // 8, peer % 8, part // 4, part % 4, tt)


WAVES = (((0, 2), (2, 4)), ((5, 6), (6, 7)))
Z_TILE = 4
FIRST = 4
SPANS = ((0, FIRST), (FIRST, 7))
LOOKS = ((0, 7), (7, 14), (14, 20), (20, 26))
T = (8, 128)


def scratch_list():
    v = pltpu.VMEM
    dma = pltpu.SemaphoreType.DMA
    items = [
        ("stacked", v((BATCH, WIDTH), BF16)), ("upstream", v((BATCH, WIDTH), BF16)), ("gated", v((BATCH, WIDTH), BF16)),
        ("up", v((WIDTH, RANK), BF16)), ("down", v((RANK, WIDTH), BF16)), ("rows", v((SLOTS, ROWW), F32)),
        ("cache", v((CACHE, ROWW), F32)), ("home", v((HOME, ROWW), F32)), ("ids_n", v((BATCH, ROWW), jnp.int32)),
        ("ids_t", v((FEAT, BATCH), jnp.int32)), ("acc_in", v((16, ROWW), F32)), ("bias_in", v((27, ROWW), F32)),
        ("dest_in", v((NG, EVICT), jnp.int32)),
        ("idb", v((FEAT, BATCH, ROWW), jnp.int32)), ("folded", v((LINE, FOLD * ROWW), BF16)),
        ("hidden", v((BATCH, RANK), BF16)), ("back", v((BATCH, RANK), BF16)), ("hidden_t", v((RANK + 16, BATCH), BF16)),
        ("rg", v((LINE, FOLD * ROWW), F32)), ("delta", v((SLOTS, ROWW), F32)),
        ("hit_buf", v((NP, HIT, ROWW), F32)), ("miss_buf", v((NG, HIT, ROWW), F32)),
        ("ev_buf", v((NG, EVICT, ROWW), F32)), ("ev_in", v((NG, EVICT, ROWW), F32)),
        ("grad", v((2, 2, 8, 2, 4, 7) + T, F32)), ("r0", v((2, 8, 2, 4, 7) + T, F32)),
        ("rc1", v((7, 2, 2, 4) + T, F32)), ("c1", v((2, 2, 4) + T, F32)), ("rc2", v((3, 4) + T, F32)),
        ("c2", v((4,) + T, F32)), ("rc3", v((3,) + T, F32)),
        ("final", v((7,) + T, F32)), ("out_all", v((2, 2, 4, 7) + T, F32)),
        ("ag_like", v((7, 7) + T, F32)), ("fw_s", dma((2,))), ("fw_r", dma((2,))), ("in_sem", dma((11,))), ("out_sem", dma((2,))), ("core_s", dma((1,))), ("core_r", dma((5,))),
    ]
    for name in ("hit", "miss", "ev", "ag0", "ag1"):
        items += [(name + "_s", dma((1,))), (name + "_r", dma((1,)))]
    for name in ("c1", "c2", "c3"):
        items += [(name + "_s", dma((1,))), (name + "_r", dma((1,)))]
    for w, ((lo, hi), _) in enumerate(WAVES):
        n = hi - lo
        k = str(w)
        items += [
            ("ra1" + k, v((6, 8, 2, n) + T, F32)), ("a1" + k, v((2, 8, 2, n) + T, F32)),
            ("rb1" + k, v((6, 4, 4, n) + T, F32)), ("b1" + k, v((8, 4, n) + T, F32)),
            ("ra2" + k, v((3, 8, n) + T, F32)), ("rb2" + k, v((3, 8, n) + T, F32)),
            ("ab" + k, v((8, 2 * n) + T, F32)), ("rab" + k, v((7, 2 * n) + T, F32)),
        ]
        for name, m in (("xa", 3), ("yb", 3), ("ya", 1), ("xb", 1), ("z", 1)):
            items += [(name + k + "_s", dma((1,))), (name + k + "_r", dma((m,)))]
    return items


class Bag:
    pass


def kernel(*refs):
    names = [
        "dense_h", "upstream_h", "ids_h", "rows_h", "acc_h", "cache_h", "home_h", "up_h", "down_h", "bias_h", "dest_h",
        "hit_send", "hit_count", "miss_send", "miss_count", "evict_slot", "evict_count",
        "next_out", "work_out", "home_out", "gup_out", "gdown_out", "gbias_out",
    ] + [name for name, _ in scratch_list()]
    b = Bag()
    for name, ref in zip(names, refs, strict=True):
        setattr(b, name, ref)
    stacked, upstream, gated, idb, rg = b.stacked, b.upstream, b.gated, b.idb, b.rg

    g = lax.axis_index("group")
    p = lax.axis_index("peer")
    core = lax.rem(g, 2)
    x = lax.rem(g // 2, 4)
    yl = g // 8
    yh = p // 8
    z = lax.rem(p, 8)
    y = yh * 2 + yl

    def at_x(c):
        return ((yl * 4 + c) * 2 + core, p)

    def at_y(c):
        return ((lax.rem(c, 2) * 4 + x) * 2 + core, (c // 2) * 8 + z)

    def at_z(c):
        return (g, yh * 8 + c)

    loads = {}
    for k, (name, src, dst) in enumerate((
        ("ids", b.ids_h, b.ids_t), ("cache", b.cache_h, b.cache), ("home", b.home_h, b.home), ("rows", b.rows_h, b.rows),
        ("dense", b.dense_h, stacked.at[:, 0:ROWW]), ("upstream", b.upstream_h, upstream),
        ("up", b.up_h, b.up), ("down", b.down_h, b.down),
        ("acc", b.acc_h, b.acc_in), ("bias", b.bias_h, b.bias_in), ("dest", b.dest_h, b.dest_in),
    )):
        loads[name] = pltpu.make_async_copy(src, dst, b.in_sem.at[k])
        loads[name].start()

    barrier = pltpu.get_barrier_semaphore()

    def greet(i, _):
        pl.semaphore_signal(barrier, inc=1, device_id=(lax.rem(g + i, NG), p), device_id_type=MESH)
        pl.semaphore_signal(barrier, inc=1, device_id=(g, lax.rem(p + i, NP)), device_id_type=MESH)
        return 0

    lax.fori_loop(1, 16, greet, 0)
    pl.semaphore_signal(
        barrier, inc=1, device_id=(((1 - yl) * 4 + x) * 2 + core, (1 - yh) * 8 + z), device_id_type=MESH
    )

    def pick(q, table, listed, counts, buf, many):
        for k in range(many):
            buf[q, pl.ds(k, 1), :] = table[pl.ds(listed[q, k], 1), :]
        keep = lax.broadcasted_iota(jnp.int32, (many, ROWW), 0) < counts[q]
        buf[q] = jnp.where(keep, buf[q], 0.0)

    def hit_copy(q, to):
        return pltpu.make_async_remote_copy(
            b.hit_buf.at[to], b.next_out.at[pl.ds(q * HIT, HIT), :], b.hit_s.at[0], b.hit_r.at[0],
            device_id=(g, to), device_id_type=MESH)

    def miss_copy(h, to):
        return pltpu.make_async_remote_copy(
            b.miss_buf.at[to], b.next_out.at[pl.ds(NP * HIT + h * HIT, HIT), :], b.miss_s.at[0], b.miss_r.at[0],
            device_id=(to, p), device_id_type=MESH)

    def pick_out(o):
        pick(lax.rem(p + o, NP), b.cache, b.hit_send, b.hit_count, b.hit_buf, HIT)
        pick(lax.rem(g + o, NG), b.home, b.miss_send, b.miss_count, b.miss_buf, HIT)
        return 0

    loads["ids"].wait()
    b.ids_n[...] = jnp.concatenate([b.ids_t[...], jnp.zeros((ROWW - FEAT, BATCH), jnp.int32)], axis=0).T
    loads["cache"].wait()
    loads["home"].wait()
    lax.fori_loop(1, 17, lambda o, _: pick_out(o), 0)
    loads["rows"].wait()
    for j in range(FOLD):
        b.folded[:, j * ROWW:(j + 1) * ROWW] = b.rows[j * LINE:(j + 1) * LINE, :].astype(BF16)
    loads["dense"].wait()
    loads["upstream"].wait()
    gated[:, 0:ROWW] = (upstream[:, 0:ROWW].astype(F32) * stacked[:, 0:ROWW].astype(F32)).astype(BF16)

    def look(lo, hi):
        lane = lax.broadcasted_iota(jnp.int32, (BATCH, ROWW), 1)
        hots = []
        for f in range(lo, hi):
            ids = jnp.broadcast_to(b.ids_n[:, f:f + 1], (BATCH, ROWW))
            idb[f] = ids
            low = ids & (LINE - 1)
            hots.append(jnp.concatenate(
                [jnp.where(low == lane + ROWW * j, 1.0, 0.0).astype(BF16) for j in range(LINE // ROWW)], axis=1))
        got = mm(jnp.concatenate(hots, axis=0), b.folded[...])
        for e, f in enumerate(range(lo, hi)):
            high = idb[f] >> 9
            part = got[e * BATCH:(e + 1) * BATCH]
            row = part[:, 0:ROWW]
            for j in range(1, FOLD):
                row = jnp.where(high == j, part[:, j * ROWW:(j + 1) * ROWW], row)
            cols = slice((f + 1) * ROWW, (f + 2) * ROWW)
            stacked[:, cols] = row.astype(BF16)
            gated[:, cols] = (upstream[:, cols].astype(F32) * row).astype(BF16)

    pl.semaphore_wait(barrier, 31)

    def send_rows(o, _):
        hit_copy(p, lax.rem(p + o, NP)).start()
        miss_copy(g, lax.rem(g + o, NG)).start()
        return 0

    lax.fori_loop(1, 16, send_rows, 0)
    own_hit = pltpu.make_async_copy(b.hit_buf.at[p], b.next_out.at[pl.ds(p * HIT, HIT), :], b.out_sem.at[0])
    own_miss = pltpu.make_async_copy(
        b.miss_buf.at[g], b.next_out.at[pl.ds(NP * HIT + g * HIT, HIT), :], b.out_sem.at[1])
    own_hit.start()
    own_miss.start()
    for lo, hi in LOOKS:
        look(lo, hi)

    grad, r0 = b.grad, b.r0
    parts = WAVES[0] + ((Z_TILE, Z_TILE + 1),) + WAVES[1]
    swaps = []
    for k, (lo, hi) in enumerate(parts):
        swaps.append(pltpu.make_async_remote_copy(
            grad.at[1 - core, :, :, :, :, lo:hi], r0.at[:, :, :, :, lo:hi], b.core_s.at[0], b.core_r.at[k],
            device_id=(g + 1 - 2 * core, p), device_id_type=MESH))

    loads["up"].wait()
    loads["down"].wait()
    blocks = [(c0, min(2, 27 - c0)) for c0 in range(0, 27, 2)]
    nil = jnp.zeros((8, ROWW), F32)

    def down_grad():
        b.hidden[...] = mm(stacked[...], b.up[...]).astype(BF16)
        b.hidden_t[0:RANK, :] = b.hidden[...].astype(F32).T.astype(BF16)
        b.hidden_t[RANK:, :] = jnp.ones((16, BATCH), BF16)
        sums = []
        for c0, n in blocks:
            d = mm(b.hidden_t[...], gated[:, c0 * ROWW:(c0 + n) * ROWW])
            for c in range(n):
                for r in range(32):
                    grad[(1,) + tile_place(r // 2, (r % 2) * 27 + c0 + c)] = (
                        d[8 * r:8 * r + 8, c * ROWW:(c + 1) * ROWW])
            sums.append(d[RANK:RANK + 8, :])
        total = jnp.concatenate(sums + [jnp.zeros((8, 256), F32)], axis=1)
        first = lax.broadcasted_iota(jnp.int32, (8, ROWW), 0) == 0
        for q in range(NP):
            start = (216 * q) // ROWW * ROWW
            piece = total[:, start:start + 384]
            if 216 * q > start:
                piece = pltpu.roll(piece, 384 - (216 * q - start), 1)
            grad[(1,) + tile_place(q, 54)] = jnp.where(first, piece[:, 0:ROWW], piece[:, ROWW:2 * ROWW])
            grad[(1,) + tile_place(q, 55)] = nil

    def up_grad():
        b.back[...] = mm(gated[...], b.down[...], ((1,), (1,))).astype(BF16)
        for c0, n in blocks:
            u = mm(stacked[:, c0 * ROWW:(c0 + n) * ROWW], b.back[...], ((0,), (0,)))
            for rr in range(16 * n):
                r = c0 * 16 + rr
                for c in range(2):
                    grad[(0,) + tile_place(r // 27, (r % 27) * 2 + c)] = (
                        u[8 * rr:8 * rr + 8, c * ROWW:(c + 1) * ROWW])
        for q in range(NP):
            grad[(0,) + tile_place(q, 54)] = nil
            grad[(0,) + tile_place(q, 55)] = nil

    @pl.when(core == 0)
    def _():
        down_grad()
        for c in swaps:
            c.start()
        up_grad()

    @pl.when(core == 1)
    def _():
        up_grad()
        for c in swaps:
            c.start()
        down_grad()

    def merge(k):
        lo, hi = parts[k]
        swaps[k].wait_recv()

        def one(q, _):
            i, j = q // 8, lax.rem(q, 8)
            r0[i, j, :, :, lo:hi] = r0[i, j, :, :, lo:hi] + grad[core, i, j, :, :, lo:hi]
            return 0

        lax.fori_loop(0, 16, one, 0)

    def terms(i, _):
        cols = pl.ds(pl.multiple_of(ROWW + i * 256, ROWW), 256)
        cross = mm(b.hidden[...], b.down[:, cols])
        bias = b.bias_in[pl.ds(1 + 2 * i, 2), :]
        bias = jnp.concatenate([bias[0:1], bias[1:2]], axis=1)
        gi = upstream[:, cols].astype(F32) * (cross + bias + 1.0)
        gi = gi + mm(b.back[...], b.up[cols, :], ((1,), (1,)))
        hots, splits = [], []
        for e in range(2):
            f = 2 * i + e
            term = gi[:, e * ROWW:(e + 1) * ROWW]
            high = idb[f] >> 9
            splits.append(jnp.concatenate(
                [jnp.where(high == j, term, 0.0).astype(BF16) for j in range(FOLD)], axis=1))
            low = b.ids_t[pl.ds(f, 1), :] & (LINE - 1)
            hots.append(jnp.where(
                lax.broadcasted_iota(jnp.int32, (LINE, BATCH), 0) == low, 1.0, 0.0).astype(BF16))
        rg[...] += mm(jnp.concatenate(hots, axis=1), jnp.concatenate(splits, axis=0))
        return 0

    def await_bytes(ref, sem):
        pltpu.make_async_copy(ref, ref, sem).wait()

    def ring4(me, dev, chunk, buf, ss, rs, put):
        right, left = lax.rem(me + 1, 4), lax.rem(me + 3, 4)
        far = lax.rem(me + 2, 4)

        def copy(src, slot, to):
            return pltpu.make_async_remote_copy(
                src, buf.at[slot], ss.at[0], rs.at[min(slot, 2)], device_id=dev(to), device_id_type=MESH)

        copies = [
            copy(chunk(far, 0), 0, right), copy(chunk(far, 1), 1, left),
            copy(chunk(right, 1), 2, right), copy(chunk(left, 0), 3, left),
            copy(chunk(right, 0), 4, right), copy(chunk(left, 1), 5, left),
        ]

        def start():
            for c in copies[:4]:
                c.start()

        def middle():
            for s, piece in ((0, chunk(right, 0)), (1, chunk(left, 1))):
                copies[s].wait_recv()
                piece[...] = piece[...] + buf[s]
                copies[4 + s].start()

        def finish():
            await_bytes(buf.at[2:6], rs.at[2])
            put(0, chunk(me, 0)[...] + buf[3] + buf[4])
            put(1, chunk(me, 1)[...] + buf[2] + buf[5])

        def done():
            await_bytes(buf, ss.at[0])

        return start, middle, finish, done

    def direct(n, me, dev, chunk, buf, ss, rs, put):
        copies = []
        for d in range(1, n):
            to = lax.rem(me + d, n)
            copies.append(pltpu.make_async_remote_copy(
                chunk(to), buf.at[d - 1], ss.at[0], rs.at[0], device_id=dev(to), device_id_type=MESH))

        def start():
            for c in copies:
                c.start()

        def finish():
            await_bytes(buf, rs.at[0])
            s = chunk(me)[...]
            for d in range(n - 1):
                s = s + buf[d]
            put(s)

        def done():
            await_bytes(buf, ss.at[0])

        return start, finish, done

    def setter(ref, at):
        def put(*v):
            ref[at(*v[:-1])] = v[-1]
        return put

    def sl(lo, hi):
        return slice(lo, hi)

    xa, yb, ya, xb, zw = [], [], [], [], []
    for w, ((alo, ahi), (blo, bhi)) in enumerate(WAVES):
        k = str(w)
        n = ahi - alo
        t = {m: getattr(b, m + k) for m in (
            "ra1", "a1", "rb1", "b1", "ra2", "rb2", "ab", "rab", "xa", "yb", "ya", "xb", "z") if hasattr(b, m + k)}
        sems = {m: (getattr(b, m + k + "_s"), getattr(b, m + k + "_r")) for m in ("xa", "yb", "ya", "xb", "z")}
        xa.append(ring4(
            x, at_x, lambda c, h, lo=alo, hi=ahi: r0.at[h, :, :, c, lo:hi], t["ra1"], *sems["xa"],
            setter(t["a1"], lambda h: h)))
        yb.append(ring4(
            y, at_y, lambda c, h, lo=blo, hi=bhi: r0.at[c // 2, 4 * h:4 * h + 4, lax.rem(c, 2), :, lo:hi],
            t["rb1"], *sems["yb"], setter(t["b1"], lambda h: sl(4 * h, 4 * h + 4))))
        ya.append(direct(
            4, y, at_y, lambda c, r=t["a1"]: r.at[c // 2, :, lax.rem(c, 2)], t["ra2"], *sems["ya"],
            setter(t["ab"], lambda n=n: (slice(None), sl(0, n)))))
        xb.append(direct(
            4, x, at_x, lambda c, r=t["b1"]: r.at[:, c], t["rb2"], *sems["xb"],
            setter(t["ab"], lambda n=n: (slice(None), sl(n, 2 * n)))))
        zw.append(direct(
            8, z, at_z, lambda c, r=t["ab"]: r.at[c], t["rab"], *sems["z"],
            setter(b.final, lambda lo=alo, hi=bhi: sl(lo, hi))))
    zc = direct(
        8, z, at_z, lambda c: r0.at[:, c, :, :, Z_TILE], b.rc1, b.c1_s, b.c1_r, setter(b.c1, lambda: Ellipsis))
    yc = direct(
        4, y, at_y, lambda c: b.c1.at[c // 2, lax.rem(c, 2)], b.rc2, b.c2_s, b.c2_r, setter(b.c2, lambda: Ellipsis))
    xc = direct(4, x, at_x, lambda c: b.c2.at[c], b.rc3, b.c3_s, b.c3_r, setter(b.final, lambda: Z_TILE))

    def ev_copy(src, to):
        return pltpu.make_async_remote_copy(
            b.ev_buf.at[to], b.ev_in.at[src], b.ev_s.at[0], b.ev_r.at[0], device_id=(to, p), device_id_type=MESH)

    def adagrad():
        acc_t = jnp.concatenate([b.acc_in[...], jnp.zeros((112, ROWW), F32)], axis=0).T
        for k in range(16):
            j, i = divmod(k, 4)
            grads = rg[i * ROWW:(i + 1) * ROWW, j * ROWW:(j + 1) * ROWW]
            new = acc_t[:, k:k + 1] + jnp.mean(grads * grads, axis=1, keepdims=True)
            step = grads * (-STEP_SIZE * lax.rsqrt(new))
            b.delta[k * ROWW:(k + 1) * ROWW, :] = step
            b.work_out[k * ROWW:(k + 1) * ROWW, :] = b.rows[k * ROWW:(k + 1) * ROWW, :] + step

    def evict():
        def one(i, _):
            pick(lax.rem(g + i, NG), b.delta, b.evict_slot, b.evict_count, b.ev_buf, EVICT)

            @pl.when(i < 16)
            def _():
                ev_copy(g, lax.rem(g + i, NG)).start()
            return 0

        lax.fori_loop(1, 17, one, 0)
        b.ev_in[g] = b.ev_buf[g]

    def settle_home():
        await_bytes(b.ev_in.at[0:NG - 1], b.ev_r.at[0])
        place = jnp.concatenate([b.dest_in[k:k + 1, :] for k in range(NG)], axis=1)
        hot = jnp.where(lax.broadcasted_iota(jnp.int32, (HOME, NG * EVICT), 0) == place, 1.0, 0.0).astype(BF16)
        b.home_out[...] = b.home[...] + mm(hot, b.ev_in[...].reshape(NG * EVICT, ROWW).astype(BF16))

    def ag_copy(w, to):
        lo, hi = SPANS[w]
        ss, rs = ((b.ag0_s, b.ag0_r), (b.ag1_s, b.ag1_r))[w]
        return pltpu.make_async_remote_copy(
            b.final.at[lo:hi], b.out_all.at[core, yl, x, lo:hi], ss.at[0], rs.at[0],
            device_id=(to * 2 + core, p), device_id_type=MESH)

    def spread(w):
        def one(i, _):
            ag_copy(w, lax.rem(yl * 4 + x + i, 8)).start()
            return 0

        lax.fori_loop(1, 8, one, 0)
        lo, hi = SPANS[w]
        b.out_all[core, yl, x, lo:hi] = b.final[lo:hi]

    pairs = []
    for w, (lo, hi) in enumerate(SPANS):
        pairs.append(pltpu.make_async_remote_copy(
            b.out_all.at[core, :, :, lo:hi], b.out_all.at[core, :, :, lo:hi], b.fw_s.at[w], b.fw_r.at[w],
            device_id=(g + 1 - 2 * core, p), device_id_type=MESH))

    def forward(w):
        lo, hi = SPANS[w]
        await_bytes(b.ag_like.at[:, lo:hi], (b.ag0_r, b.ag1_r)[w].at[0])
        pairs[w].start()

    def run_terms(lo, hi):
        lax.fori_loop(lo, hi, terms, 0)

    loads["acc"].wait()
    loads["bias"].wait()
    loads["dest"].wait()
    rg[...] = jnp.zeros_like(rg)
    merge(0)
    xa[0][0]()
    run_terms(0, 1)
    merge(1)
    yb[0][0]()
    run_terms(1, 2)
    merge(2)
    zc[0]()
    run_terms(2, 3)
    merge(3)
    xa[1][0]()
    merge(4)
    yb[1][0]()
    run_terms(3, 6)
    xa[0][1]()
    run_terms(6, 7)
    yb[0][1]()
    run_terms(7, 9)
    xa[1][1]()
    run_terms(9, 10)
    yb[1][1]()
    run_terms(10, 12)
    xa[0][2]()
    ya[0][0]()
    run_terms(12, 13)
    yb[0][2]()
    xb[0][0]()
    xa[1][2]()
    ya[1][0]()
    yb[1][2]()
    xb[1][0]()
    zc[1]()
    yc[0]()
    adagrad()
    evict()
    ya[0][1]()
    xb[0][1]()
    zw[0][0]()
    ya[1][1]()
    xb[1][1]()
    zw[1][0]()
    yc[1]()
    xc[0]()
    zw[0][1]()
    spread(0)
    zw[1][1]()
    xc[1]()
    spread(1)
    forward(0)
    settle_home()
    forward(1)

    for sems in ((b.hit_s, b.hit_r), (b.miss_s, b.miss_r)):
        for sem in sems:
            await_bytes(b.hit_buf.at[0:NP - 1], sem.at[0])
    await_bytes(b.ev_buf.at[0:NG - 1], b.ev_s.at[0])
    await_bytes(r0, b.core_s.at[0])
    for phase in xa + yb + ya + xb + zw + [zc, yc, xc]:
        phase[-1]()
    own_hit.wait()
    own_miss.wait()
    for (lo, hi), sem, pair in zip(SPANS, (b.ag0_s, b.ag1_s), pairs):
        await_bytes(b.ag_like.at[:, lo:hi], sem.at[0])
        pair.wait_send()
        pair.wait_recv()

    def tile(c, t):
        part, tt = divmod(t, 7)
        return b.out_all[c, part // 4, part % 4, tt]

    for r in range(27):
        for c in range(2):
            b.gup_out[8 * r:8 * r + 8, c * ROWW:(c + 1) * ROWW] = tile(0, 2 * r + c)
    for r in range(2):
        for c in range(27):
            b.gdown_out[8 * r:8 * r + 8, c * ROWW:(c + 1) * ROWW] = tile(1, 27 * r + c)
    b.gbias_out[...] = tile(1, 54)


PIECES = (4, 4, 2, 1, 1)


def hand_on(n_in, w_in, h_in, u_in, d_in, b_in, n_out, w_out, h_out, u_out, d_out, b_out, sems):
    copies = []
    for k, (src, dst) in enumerate(zip((n_in, w_in, h_in, u_in, d_in), (n_out, w_out, h_out, u_out, d_out))):
        pieces = PIECES[k]
        size = src.shape[0] // pieces
        for i in range(pieces):
            rows = pl.ds(i * size, size)
            pltpu.make_async_copy(src.at[rows], dst.at[rows], sems.at[k]).start()
        copies.append(pltpu.make_async_copy(src, dst, sems.at[k]))
    b_out[0:ROWW] = b_in[0]
    b_out[ROWW:216] = b_in[1, 0:216 - ROWW]
    for c in copies:
        c.wait()


def body(
    dense_feat, upstream, cur_ids, work_rows, work_acc, cache_table, home_table, hit_send, hit_count,
    miss_send, miss_count, evict_slot, evict_dest, evict_count, up_proj, down_proj, cross_bias,
):
    vmem = pl.BlockSpec(memory_space=pltpu.VMEM)
    smem = pl.BlockSpec(memory_space=pltpu.SMEM)
    anyw = pl.BlockSpec(memory_space=pl.ANY)
    shapes = [
        jax.ShapeDtypeStruct(s, F32)
        for s in ((SLOTS, ROWW), (SLOTS, ROWW), (HOME, ROWW), (216, RANK), (16, WIDTH), (8, ROWW))
    ]
    out = pl.pallas_call(
        kernel,
        out_shape=tuple(pltpu.VMEM(s.shape, F32) for s in shapes),
        in_specs=[anyw] * 11 + [smem] * 6,
        out_specs=(vmem,) * 6,
        scratch_shapes=[s for _, s in scratch_list()],
        compiler_params=pltpu.CompilerParams(
            collective_id=0, has_side_effects=True, vmem_limit_bytes=60 * 1024 * 1024),
        name="cross_step",
    )(
        dense_feat, upstream, cur_ids.T, work_rows, work_acc.reshape(16, ROWW), cache_table, home_table,
        up_proj, down_proj, cross_bias.reshape(27, ROWW), evict_dest,
        hit_send, hit_count, miss_send, miss_count, evict_slot, evict_count,
    )
    return pl.pallas_call(
        hand_on,
        out_shape=tuple(shapes[:5]) + (jax.ShapeDtypeStruct((216,), F32),),
        in_specs=[vmem] * 6,
        out_specs=(anyw,) * 5 + (vmem,),
        scratch_shapes=[pltpu.SemaphoreType.DMA((5,))],
        compiler_params=pltpu.CompilerParams(vmem_limit_bytes=4 * 1024 * 1024),
        name="hand_on",
    )(*[pltpu.with_memory_space_constraint(o, pltpu.VMEM) for o in out])


def solution(mesh):
    rows = P(("group", "peer"), None)
    flat = P(("group", "peer"))
    return jax.shard_map(
        body,
        mesh=mesh,
        in_specs=(rows, rows, rows, rows, flat, rows, rows, rows, flat, rows, flat, rows, rows, flat, P(), P(), P()),
        out_specs=(rows, rows, rows, P("peer", None), P("peer", None), P("peer")),
        check_vma=False,
    )
```

```python
import jax
import jax.numpy as jnp
from jax import lax
from jax.experimental import pallas as pl
from jax.experimental.pallas import tpu as pltpu
from jax.sharding import PartitionSpec as P

MESH = pl.DeviceIdType.MESH
F32 = jnp.float32
BF16 = jnp.bfloat16

ROWW = 128
FEAT = 26
RANK = 256
BATCH = 384
WIDTH = 3456
SLOTS = 2048
HOME = 1024
CACHE = 512
HIT = 64
EVICT = 32
FOLD = 4
LINE = SLOTS // FOLD
NG = 16
NP = 16
STEP_SIZE = 0.5


def mm(a, b, dims=((1,), (0,))):
    return lax.dot_general(a, b, (dims, ((), ())), preferred_element_type=F32)


def tile_place(peer, t):
    part, tt = divmod(t, 7)
    yh, z, yl, x = peer // 8, peer % 8, part // 4, part % 4
    for k, (lo, hi) in enumerate(PARTS):
        if lo <= tt < hi:
            place = ((x, yh, z, yl), (yh, yl, z, x), (z, yh, yl, x))[KINDS[k]]
            return k, place + (tt - lo,)


WAVES = (((0, 2), (2, 4)), ((5, 6), (6, 7)))
Z_TILE = 4
FIRST = 4
PARTS = WAVES[0] + ((Z_TILE, Z_TILE + 1),) + WAVES[1]
KINDS = (0, 1, 2, 0, 1)
DIMS = ((4, 2, 8, 2), (2, 2, 8, 4), (8, 2, 2, 4))
SPANS = ((0, FIRST), (FIRST, 7))
LOOKS = ((0, 7), (7, 14), (14, 20), (20, 26))
T = (8, 128)


def scratch_list():
    v = pltpu.VMEM
    dma = pltpu.SemaphoreType.DMA
    items = [
        ("stacked", v((BATCH, WIDTH), BF16)), ("upstream", v((BATCH, WIDTH), BF16)), ("gated", v((BATCH, WIDTH), BF16)),
        ("up", v((WIDTH, RANK), BF16)), ("down", v((RANK, WIDTH), BF16)), ("rows", v((SLOTS, ROWW), F32)),
        ("cache", v((CACHE, ROWW), F32)), ("home", v((HOME, ROWW), F32)), ("ids_n", v((BATCH, ROWW), jnp.int32)),
        ("ids_t", v((FEAT, BATCH), jnp.int32)), ("acc_in", v((16, ROWW), F32)), ("bias_in", v((27, ROWW), F32)),
        ("dest_in", v((NG, EVICT), jnp.int32)),
        ("idb", v((FEAT, BATCH, ROWW), jnp.int32)), ("folded", v((LINE, FOLD * ROWW), BF16)),
        ("hidden", v((BATCH, RANK), BF16)), ("back", v((BATCH, RANK), BF16)), ("hidden_t", v((RANK + 16, BATCH), BF16)),
        ("rg", v((LINE, FOLD * ROWW), F32)), ("delta", v((SLOTS, ROWW), F32)),
        ("hit_buf", v((NP, HIT, ROWW), F32)), ("miss_buf", v((NG, HIT, ROWW), F32)),
        ("ev_buf", v((NG, EVICT, ROWW), F32)), ("ev_in", v((NG, EVICT, ROWW), F32)),
        ("rc1", v((7, 2, 2, 4) + T, F32)), ("c1", v((2, 2, 4) + T, F32)), ("rc2", v((3, 4) + T, F32)),
        ("c2", v((4,) + T, F32)), ("rc3", v((3,) + T, F32)),
        ("final", v((7,) + T, F32)), ("out_all", v((2, 2, 4, 7) + T, F32)),
        ("ag_like", v((7, 7) + T, F32)), ("fw_s", dma((2,))), ("fw_r", dma((2,))), ("in_sem", dma((11,))), ("out_sem", dma((2,))), ("core_s", dma((5,))), ("core_r", dma((5,))),
    ]
    for k, (lo, hi) in enumerate(PARTS):
        dims = DIMS[KINDS[k]] + (hi - lo,) + T
        items += [("grad" + str(k), v((2,) + dims, F32)), ("r0" + str(k), v(dims, F32))]
    for name in ("hit", "miss", "ev", "ag0", "ag1"):
        items += [(name + "_s", dma((1,))), (name + "_r", dma((1,)))]
    for name in ("c1", "c2", "c3"):
        items += [(name + "_s", dma((1,))), (name + "_r", dma((1,)))]
    for w, ((lo, hi), _) in enumerate(WAVES):
        n = hi - lo
        k = str(w)
        items += [
            ("ra1" + k, v((6, 8, 2, n) + T, F32)), ("a1" + k, v((2, 2, 8, n) + T, F32)),
            ("rb1" + k, v((6, 4, 4, n) + T, F32)), ("b1" + k, v((4, 8, n) + T, F32)),
            ("ra2" + k, v((3, 8, n) + T, F32)), ("rb2" + k, v((3, 8, n) + T, F32)),
            ("ab" + k, v((8, 2 * n) + T, F32)), ("rab" + k, v((7, 2 * n) + T, F32)),
        ]
        for name, m in (("xa", 3), ("yb", 3), ("ya", 1), ("xb", 1), ("z", 1)):
            items += [(name + k + "_s", dma((1,))), (name + k + "_r", dma((m,)))]
    return items


class Bag:
    pass


def kernel(*refs):
    names = [
        "dense_h", "upstream_h", "ids_h", "rows_h", "acc_h", "cache_h", "home_h", "up_h", "down_h", "bias_h", "dest_h",
        "hit_send", "hit_count", "miss_send", "miss_count", "evict_slot", "evict_count",
        "next_out", "work_out", "home_out", "gup_out", "gdown_out", "gbias_out",
    ] + [name for name, _ in scratch_list()]
    b = Bag()
    for name, ref in zip(names, refs, strict=True):
        setattr(b, name, ref)
    stacked, upstream, gated, idb, rg = b.stacked, b.upstream, b.gated, b.idb, b.rg

    g = lax.axis_index("group")
    p = lax.axis_index("peer")
    core = lax.rem(g, 2)
    x = lax.rem(g // 2, 4)
    yl = g // 8
    yh = p // 8
    z = lax.rem(p, 8)
    y = yh * 2 + yl

    def at_x(c):
        return ((yl * 4 + c) * 2 + core, p)

    def at_y(c):
        return ((lax.rem(c, 2) * 4 + x) * 2 + core, (c // 2) * 8 + z)

    def at_z(c):
        return (g, yh * 8 + c)

    loads = {}
    for k, (name, src, dst) in enumerate((
        ("ids", b.ids_h, b.ids_t), ("cache", b.cache_h, b.cache), ("home", b.home_h, b.home), ("rows", b.rows_h, b.rows),
        ("dense", b.dense_h, stacked.at[:, 0:ROWW]), ("upstream", b.upstream_h, upstream),
        ("up", b.up_h, b.up), ("down", b.down_h, b.down),
        ("acc", b.acc_h, b.acc_in), ("bias", b.bias_h, b.bias_in), ("dest", b.dest_h, b.dest_in),
    )):
        loads[name] = pltpu.make_async_copy(src, dst, b.in_sem.at[k])
        loads[name].start()

    barrier = pltpu.get_barrier_semaphore()

    def greet(i, _):
        pl.semaphore_signal(barrier, inc=1, device_id=(lax.rem(g + i, NG), p), device_id_type=MESH)
        pl.semaphore_signal(barrier, inc=1, device_id=(g, lax.rem(p + i, NP)), device_id_type=MESH)
        return 0

    lax.fori_loop(1, 16, greet, 0)
    pl.semaphore_signal(
        barrier, inc=1, device_id=(((1 - yl) * 4 + x) * 2 + core, (1 - yh) * 8 + z), device_id_type=MESH
    )

    def pick(q, table, listed, counts, buf, many):
        for k in range(many):
            buf[q, pl.ds(k, 1), :] = table[pl.ds(listed[q, k], 1), :]
        keep = lax.broadcasted_iota(jnp.int32, (many, ROWW), 0) < counts[q]
        buf[q] = jnp.where(keep, buf[q], 0.0)

    def hit_copy(q, to):
        return pltpu.make_async_remote_copy(
            b.hit_buf.at[to], b.next_out.at[pl.ds(q * HIT, HIT), :], b.hit_s.at[0], b.hit_r.at[0],
            device_id=(g, to), device_id_type=MESH)

    def miss_copy(h, to):
        return pltpu.make_async_remote_copy(
            b.miss_buf.at[to], b.next_out.at[pl.ds(NP * HIT + h * HIT, HIT), :], b.miss_s.at[0], b.miss_r.at[0],
            device_id=(to, p), device_id_type=MESH)

    def pick_out(o):
        pick(lax.rem(p + o, NP), b.cache, b.hit_send, b.hit_count, b.hit_buf, HIT)
        pick(lax.rem(g + o, NG), b.home, b.miss_send, b.miss_count, b.miss_buf, HIT)
        return 0

    loads["ids"].wait()
    b.ids_n[...] = jnp.concatenate([b.ids_t[...], jnp.zeros((ROWW - FEAT, BATCH), jnp.int32)], axis=0).T
    loads["cache"].wait()
    loads["home"].wait()
    lax.fori_loop(1, 17, lambda o, _: pick_out(o), 0)
    loads["rows"].wait()
    for j in range(FOLD):
        b.folded[:, j * ROWW:(j + 1) * ROWW] = b.rows[j * LINE:(j + 1) * LINE, :].astype(BF16)
    loads["dense"].wait()
    loads["upstream"].wait()
    gated[:, 0:ROWW] = (upstream[:, 0:ROWW].astype(F32) * stacked[:, 0:ROWW].astype(F32)).astype(BF16)

    def look(lo, hi):
        lane = lax.broadcasted_iota(jnp.int32, (BATCH, ROWW), 1)
        hots = []
        for f in range(lo, hi):
            ids = jnp.broadcast_to(b.ids_n[:, f:f + 1], (BATCH, ROWW))
            idb[f] = ids
            low = ids & (LINE - 1)
            hots.append(jnp.concatenate(
                [jnp.where(low == lane + ROWW * j, 1.0, 0.0).astype(BF16) for j in range(LINE // ROWW)], axis=1))
        got = mm(jnp.concatenate(hots, axis=0), b.folded[...])
        for e, f in enumerate(range(lo, hi)):
            high = idb[f] >> 9
            part = got[e * BATCH:(e + 1) * BATCH]
            row = part[:, 0:ROWW]
            for j in range(1, FOLD):
                row = jnp.where(high == j, part[:, j * ROWW:(j + 1) * ROWW], row)
            cols = slice((f + 1) * ROWW, (f + 2) * ROWW)
            stacked[:, cols] = row.astype(BF16)
            gated[:, cols] = (upstream[:, cols].astype(F32) * row).astype(BF16)

    pl.semaphore_wait(barrier, 31)

    def send_rows(o, _):
        hit_copy(p, lax.rem(p + o, NP)).start()
        miss_copy(g, lax.rem(g + o, NG)).start()
        return 0

    lax.fori_loop(1, 16, send_rows, 0)
    own_hit = pltpu.make_async_copy(b.hit_buf.at[p], b.next_out.at[pl.ds(p * HIT, HIT), :], b.out_sem.at[0])
    own_miss = pltpu.make_async_copy(
        b.miss_buf.at[g], b.next_out.at[pl.ds(NP * HIT + g * HIT, HIT), :], b.out_sem.at[1])
    own_hit.start()
    own_miss.start()
    for lo, hi in LOOKS:
        look(lo, hi)

    grads_of = [getattr(b, "grad" + str(k)) for k in range(5)]
    r0s = [getattr(b, "r0" + str(k)) for k in range(5)]

    def store(array, peer, t, value):
        k, place = tile_place(peer, t)
        grads_of[k][(array,) + place] = value

    swaps = []
    for k in range(5):
        swaps.append(pltpu.make_async_remote_copy(
            grads_of[k].at[1 - core], r0s[k], b.core_s.at[k], b.core_r.at[k],
            device_id=(g + 1 - 2 * core, p), device_id_type=MESH))

    loads["up"].wait()
    loads["down"].wait()
    blocks = [(c0, min(2, 27 - c0)) for c0 in range(0, 27, 2)]
    nil = jnp.zeros((8, ROWW), F32)

    def down_grad():
        b.hidden[...] = mm(stacked[...], b.up[...]).astype(BF16)
        b.hidden_t[0:RANK, :] = b.hidden[...].astype(F32).T.astype(BF16)
        b.hidden_t[RANK:, :] = jnp.ones((16, BATCH), BF16)
        sums = []
        for c0, n in blocks:
            d = mm(b.hidden_t[...], gated[:, c0 * ROWW:(c0 + n) * ROWW])
            for c in range(n):
                for r in range(32):
                    store(1, r // 2, (r % 2) * 27 + c0 + c, d[8 * r:8 * r + 8, c * ROWW:(c + 1) * ROWW])
            sums.append(d[RANK:RANK + 8, :])
        total = jnp.concatenate(sums + [jnp.zeros((8, 256), F32)], axis=1)
        first = lax.broadcasted_iota(jnp.int32, (8, ROWW), 0) == 0
        for q in range(NP):
            start = (216 * q) // ROWW * ROWW
            piece = total[:, start:start + 384]
            if 216 * q > start:
                piece = pltpu.roll(piece, 384 - (216 * q - start), 1)
            store(1, q, 54, jnp.where(first, piece[:, 0:ROWW], piece[:, ROWW:2 * ROWW]))
            store(1, q, 55, nil)

    def up_grad():
        b.back[...] = mm(gated[...], b.down[...], ((1,), (1,))).astype(BF16)
        for c0, n in blocks:
            u = mm(stacked[:, c0 * ROWW:(c0 + n) * ROWW], b.back[...], ((0,), (0,)))
            for rr in range(16 * n):
                r = c0 * 16 + rr
                for c in range(2):
                    store(0, r // 27, (r % 27) * 2 + c, u[8 * rr:8 * rr + 8, c * ROWW:(c + 1) * ROWW])
        for q in range(NP):
            store(0, q, 54, nil)
            store(0, q, 55, nil)

    @pl.when(core == 0)
    def _():
        down_grad()
        for c in swaps:
            c.start()
        up_grad()

    @pl.when(core == 1)
    def _():
        up_grad()
        for c in swaps:
            c.start()
        down_grad()

    def merge(k):
        swaps[k].wait_recv()
        mine, other = r0s[k], grads_of[k]
        inner = mine.shape[1]

        def one(q, _):
            i, j = q // inner, lax.rem(q, inner)
            mine[i, j] = mine[i, j] + other[core, i, j]
            return 0

        lax.fori_loop(0, mine.shape[0] * inner, one, 0)

    def terms(i, _):
        cols = pl.ds(pl.multiple_of(ROWW + i * 256, ROWW), 256)
        cross = mm(b.hidden[...], b.down[:, cols])
        bias = b.bias_in[pl.ds(1 + 2 * i, 2), :]
        bias = jnp.concatenate([bias[0:1], bias[1:2]], axis=1)
        gi = upstream[:, cols].astype(F32) * (cross + bias + 1.0)
        gi = gi + mm(b.back[...], b.up[cols, :], ((1,), (1,)))
        hots, splits = [], []
        for e in range(2):
            f = 2 * i + e
            term = gi[:, e * ROWW:(e + 1) * ROWW]
            high = idb[f] >> 9
            splits.append(jnp.concatenate(
                [jnp.where(high == j, term, 0.0).astype(BF16) for j in range(FOLD)], axis=1))
            low = b.ids_t[pl.ds(f, 1), :] & (LINE - 1)
            hots.append(jnp.where(
                lax.broadcasted_iota(jnp.int32, (LINE, BATCH), 0) == low, 1.0, 0.0).astype(BF16))
        rg[...] += mm(jnp.concatenate(hots, axis=1), jnp.concatenate(splits, axis=0))
        return 0

    def await_bytes(ref, sem):
        pltpu.make_async_copy(ref, ref, sem).wait()

    def ring4(me, dev, chunk, buf, ss, rs, put):
        right, left = lax.rem(me + 1, 4), lax.rem(me + 3, 4)
        far = lax.rem(me + 2, 4)

        def copy(src, slot, to):
            return pltpu.make_async_remote_copy(
                src, buf.at[slot], ss.at[0], rs.at[min(slot, 2)], device_id=dev(to), device_id_type=MESH)

        copies = [
            copy(chunk(far, 0), 0, right), copy(chunk(far, 1), 1, left),
            copy(chunk(right, 1), 2, right), copy(chunk(left, 0), 3, left),
            copy(chunk(right, 0), 4, right), copy(chunk(left, 1), 5, left),
        ]

        def far_out():
            for c in copies[:2]:
                c.start()

        def near_out():
            for c in copies[2:4]:
                c.start()

        def middle():
            for s, piece in ((0, chunk(right, 0)), (1, chunk(left, 1))):
                copies[s].wait_recv()
                piece[...] = piece[...] + buf[s]
                copies[4 + s].start()

        def finish():
            await_bytes(buf.at[2:6], rs.at[2])
            put(0, chunk(me, 0)[...] + buf[3] + buf[4])
            put(1, chunk(me, 1)[...] + buf[2] + buf[5])

        def done():
            await_bytes(buf, ss.at[0])

        return far_out, near_out, middle, finish, done

    def direct(n, me, dev, chunk, buf, ss, rs, put):
        copies = []
        for d in sorted(range(1, n), key=lambda d: -min(d, n - d)):
            to = lax.rem(me + d, n)
            copies.append(pltpu.make_async_remote_copy(
                chunk(to), buf.at[d - 1], ss.at[0], rs.at[0], device_id=dev(to), device_id_type=MESH))

        def start():
            for c in copies:
                c.start()

        def finish():
            await_bytes(buf, rs.at[0])
            s = chunk(me)[...]
            for d in range(n - 1):
                s = s + buf[d]
            put(s)

        def done():
            await_bytes(buf, ss.at[0])

        return start, finish, done

    def setter(ref, at):
        def put(*v):
            ref[at(*v[:-1])] = v[-1]
        return put

    def sl(lo, hi):
        return slice(lo, hi)

    xa, yb, ya, xb, zw = [], [], [], [], []
    for w, ((alo, ahi), (blo, bhi)) in enumerate(WAVES):
        k = str(w)
        n = ahi - alo
        t = {m: getattr(b, m + k) for m in (
            "ra1", "a1", "rb1", "b1", "ra2", "rb2", "ab", "rab", "xa", "yb", "ya", "xb", "z") if hasattr(b, m + k)}
        sems = {m: (getattr(b, m + k + "_s"), getattr(b, m + k + "_r")) for m in ("xa", "yb", "ya", "xb", "z")}

        def put_a1(h, value, r=t["a1"]):
            for c in range(2):
                r[h, c] = value[:, c]

        def put_b1(h, value, r=t["b1"]):
            for c in range(4):
                r[c, 4 * h:4 * h + 4] = value[:, c]

        xa.append(ring4(
            x, at_x, lambda c, h, r=r0s[3 * w]: r.at[c, h], t["ra1"], *sems["xa"], put_a1))
        yb.append(ring4(
            y, at_y, lambda c, h, r=r0s[3 * w + 1]: r.at[c // 2, lax.rem(c, 2), 4 * h:4 * h + 4],
            t["rb1"], *sems["yb"], put_b1))
        ya.append(direct(
            4, y, at_y, lambda c, r=t["a1"]: r.at[c // 2, lax.rem(c, 2)], t["ra2"], *sems["ya"],
            setter(t["ab"], lambda n=n: (slice(None), sl(0, n)))))
        xb.append(direct(
            4, x, at_x, lambda c, r=t["b1"]: r.at[c], t["rb2"], *sems["xb"],
            setter(t["ab"], lambda n=n: (slice(None), sl(n, 2 * n)))))
        zw.append(direct(
            8, z, at_z, lambda c, r=t["ab"]: r.at[c], t["rab"], *sems["z"],
            setter(b.final, lambda lo=alo, hi=bhi: sl(lo, hi))))
    zc = direct(
        8, z, at_z, lambda c: r0s[2].at[c, :, :, :, 0], b.rc1, b.c1_s, b.c1_r, setter(b.c1, lambda: Ellipsis))
    yc = direct(
        4, y, at_y, lambda c: b.c1.at[c // 2, lax.rem(c, 2)], b.rc2, b.c2_s, b.c2_r, setter(b.c2, lambda: Ellipsis))
    xc = direct(4, x, at_x, lambda c: b.c2.at[c], b.rc3, b.c3_s, b.c3_r, setter(b.final, lambda: Z_TILE))

    def ev_copy(src, to):
        return pltpu.make_async_remote_copy(
            b.ev_buf.at[to], b.ev_in.at[src], b.ev_s.at[0], b.ev_r.at[0], device_id=(to, p), device_id_type=MESH)

    def adagrad():
        acc_t = jnp.concatenate([b.acc_in[...], jnp.zeros((112, ROWW), F32)], axis=0).T
        for k in range(16):
            j, i = divmod(k, 4)
            grads = rg[i * ROWW:(i + 1) * ROWW, j * ROWW:(j + 1) * ROWW]
            new = acc_t[:, k:k + 1] + jnp.mean(grads * grads, axis=1, keepdims=True)
            step = grads * (-STEP_SIZE * lax.rsqrt(new))
            b.delta[k * ROWW:(k + 1) * ROWW, :] = step
            b.work_out[k * ROWW:(k + 1) * ROWW, :] = b.rows[k * ROWW:(k + 1) * ROWW, :] + step

    def evict():
        def one(i, _):
            pick(lax.rem(g + i, NG), b.delta, b.evict_slot, b.evict_count, b.ev_buf, EVICT)

            @pl.when(i < 16)
            def _():
                ev_copy(g, lax.rem(g + i, NG)).start()
            return 0

        lax.fori_loop(1, 17, one, 0)
        b.ev_in[g] = b.ev_buf[g]

    def settle_home():
        await_bytes(b.ev_in.at[0:NG - 1], b.ev_r.at[0])
        place = jnp.concatenate([b.dest_in[k:k + 1, :] for k in range(NG)], axis=1)
        hot = jnp.where(lax.broadcasted_iota(jnp.int32, (HOME, NG * EVICT), 0) == place, 1.0, 0.0).astype(BF16)
        b.home_out[...] = b.home[...] + mm(hot, b.ev_in[...].reshape(NG * EVICT, ROWW).astype(BF16))

    def ag_copy(w, to):
        lo, hi = SPANS[w]
        ss, rs = ((b.ag0_s, b.ag0_r), (b.ag1_s, b.ag1_r))[w]
        return pltpu.make_async_remote_copy(
            b.final.at[lo:hi], b.out_all.at[core, yl, x, lo:hi], ss.at[0], rs.at[0],
            device_id=(to * 2 + core, p), device_id_type=MESH)

    def spread(w):
        def one(i, _):
            ag_copy(w, lax.rem(yl * 4 + x + i, 8)).start()
            return 0

        lax.fori_loop(1, 8, one, 0)
        lo, hi = SPANS[w]
        b.out_all[core, yl, x, lo:hi] = b.final[lo:hi]

    pairs = []
    for w, (lo, hi) in enumerate(SPANS):
        pairs.append(pltpu.make_async_remote_copy(
            b.out_all.at[core, :, :, lo:hi], b.out_all.at[core, :, :, lo:hi], b.fw_s.at[w], b.fw_r.at[w],
            device_id=(g + 1 - 2 * core, p), device_id_type=MESH))

    def forward(w):
        lo, hi = SPANS[w]
        await_bytes(b.ag_like.at[:, lo:hi], (b.ag0_r, b.ag1_r)[w].at[0])
        pairs[w].start()

    def run_terms(lo, hi):
        lax.fori_loop(lo, hi, terms, 0)

    loads["acc"].wait()
    loads["bias"].wait()
    loads["dest"].wait()
    rg[...] = jnp.zeros_like(rg)
    merge(0)
    xa[0][0]()
    run_terms(0, 1)
    merge(1)
    yb[0][0]()
    run_terms(1, 2)
    merge(2)
    zc[0]()
    merge(3)
    xa[1][0]()
    xa[0][1]()
    xa[1][1]()
    merge(4)
    yb[1][0]()
    yb[0][1]()
    yb[1][1]()
    run_terms(2, 5)
    xa[0][2]()
    run_terms(5, 6)
    yb[0][2]()
    run_terms(6, 7)
    xa[1][2]()
    run_terms(7, 8)
    yb[1][2]()
    run_terms(8, 12)
    xa[0][3]()
    ya[0][0]()
    yb[0][3]()
    xb[0][0]()
    run_terms(12, 13)
    xa[1][3]()
    ya[1][0]()
    yb[1][3]()
    xb[1][0]()
    zc[1]()
    yc[0]()
    adagrad()
    evict()
    ya[0][1]()
    xb[0][1]()
    zw[0][0]()
    ya[1][1]()
    xb[1][1]()
    zw[1][0]()
    yc[1]()
    xc[0]()
    zw[0][1]()
    spread(0)
    zw[1][1]()
    xc[1]()
    spread(1)
    forward(0)
    settle_home()
    forward(1)

    for sems in ((b.hit_s, b.hit_r), (b.miss_s, b.miss_r)):
        for sem in sems:
            await_bytes(b.hit_buf.at[0:NP - 1], sem.at[0])
    await_bytes(b.ev_buf.at[0:NG - 1], b.ev_s.at[0])
    for c in swaps:
        c.wait_send()
    for phase in xa + yb + ya + xb + zw + [zc, yc, xc]:
        phase[-1]()
    own_hit.wait()
    own_miss.wait()
    for (lo, hi), sem, pair in zip(SPANS, (b.ag0_s, b.ag1_s), pairs):
        await_bytes(b.ag_like.at[:, lo:hi], sem.at[0])
        pair.wait_send()
        pair.wait_recv()

    def tile(c, t):
        part, tt = divmod(t, 7)
        return b.out_all[c, part // 4, part % 4, tt]

    for r in range(27):
        for c in range(2):
            b.gup_out[8 * r:8 * r + 8, c * ROWW:(c + 1) * ROWW] = tile(0, 2 * r + c)
    for r in range(2):
        for c in range(27):
            b.gdown_out[8 * r:8 * r + 8, c * ROWW:(c + 1) * ROWW] = tile(1, 27 * r + c)
    b.gbias_out[...] = tile(1, 54)


PIECES = (4, 4, 2, 1, 1)


def hand_on(n_in, w_in, h_in, u_in, d_in, b_in, n_out, w_out, h_out, u_out, d_out, b_out, sems):
    copies = []
    for k, (src, dst) in enumerate(zip((n_in, w_in, h_in, u_in, d_in), (n_out, w_out, h_out, u_out, d_out))):
        pieces = PIECES[k]
        size = src.shape[0] // pieces
        for i in range(pieces):
            rows = pl.ds(i * size, size)
            pltpu.make_async_copy(src.at[rows], dst.at[rows], sems.at[k]).start()
        copies.append(pltpu.make_async_copy(src, dst, sems.at[k]))
    b_out[0:ROWW] = b_in[0]
    b_out[ROWW:216] = b_in[1, 0:216 - ROWW]
    for c in copies:
        c.wait()


def body(
    dense_feat, upstream, cur_ids, work_rows, work_acc, cache_table, home_table, hit_send, hit_count,
    miss_send, miss_count, evict_slot, evict_dest, evict_count, up_proj, down_proj, cross_bias,
):
    vmem = pl.BlockSpec(memory_space=pltpu.VMEM)
    smem = pl.BlockSpec(memory_space=pltpu.SMEM)
    anyw = pl.BlockSpec(memory_space=pl.ANY)
    shapes = [
        jax.ShapeDtypeStruct(s, F32)
        for s in ((SLOTS, ROWW), (SLOTS, ROWW), (HOME, ROWW), (216, RANK), (16, WIDTH), (8, ROWW))
    ]
    out = pl.pallas_call(
        kernel,
        out_shape=tuple(pltpu.VMEM(s.shape, F32) for s in shapes),
        in_specs=[anyw] * 11 + [smem] * 6,
        out_specs=(vmem,) * 6,
        scratch_shapes=[s for _, s in scratch_list()],
        compiler_params=pltpu.CompilerParams(
            collective_id=0, has_side_effects=True, vmem_limit_bytes=60 * 1024 * 1024),
        name="cross_step",
    )(
        dense_feat, upstream, cur_ids.T, work_rows, work_acc.reshape(16, ROWW), cache_table, home_table,
        up_proj, down_proj, cross_bias.reshape(27, ROWW), evict_dest,
        hit_send, hit_count, miss_send, miss_count, evict_slot, evict_count,
    )
    return pl.pallas_call(
        hand_on,
        out_shape=tuple(shapes[:5]) + (jax.ShapeDtypeStruct((216,), F32),),
        in_specs=[vmem] * 6,
        out_specs=(anyw,) * 5 + (vmem,),
        scratch_shapes=[pltpu.SemaphoreType.DMA((5,))],
        compiler_params=pltpu.CompilerParams(vmem_limit_bytes=4 * 1024 * 1024),
        name="hand_on",
    )(*[pltpu.with_memory_space_constraint(o, pltpu.VMEM) for o in out])


def solution(mesh):
    rows = P(("group", "peer"), None)
    flat = P(("group", "peer"))
    return jax.shard_map(
        body,
        mesh=mesh,
        in_specs=(rows, rows, rows, rows, flat, rows, rows, rows, flat, rows, flat, rows, rows, flat, P(), P(), P()),
        out_specs=(rows, rows, rows, P("peer", None), P("peer", None), P("peer")),
        check_vma=False,
    )
```
